256 devices in a mesh: row: 16 (over y, x_lo, core), col: 16 (over z, x_hi).
Axes of the slice: x: 4 (x_hi: 2, x_lo: 2; x = x_hi * 2 + x_lo), y: 4, z: 8, core: 2. Of those that a mesh axis runs over, the one named last changes fastest.
Arguments:
- node_feats: bfloat16 [524288, 128], P(('row', 'col')), may hold values from -6 to 6
- tile_vals: bfloat16 [16, 16, 256, 128, 128], P('row', 'col'), as said below
- tile_dest: int32 [16, 16, 256], P('row', 'col'), may hold values from 0 to 255, as said below
- tile_source: int32 [16, 16, 256], P('row', 'col'), may hold values from 0 to 255, as said below
- tile_count: int32 [16, 16], P('row', 'col'), may hold values from 32 to 256, as said below
- weight: bfloat16 [128, 256], replicated, may hold values from -0.5 to 0.5
- out_bias: float32 [256], replicated, may hold values from -3 to 3
Outputs:
- layer_out: bfloat16 [524288, 256], P(('row', 'col'))
The draws below stay inside these ranges and needn't reach their ends.
Inputs may be any that keep to these rules, and one draw needn't show every extreme that they name: `tile_count`: busiest device holds exactly 256 live tiles in every draw; the loads follow a power law. `tile_dest`: 0 in slots at or past the device's count. The live tiles of one device touch at most 8 distinct destination blocks among the 16 blocks of each index of col, and some device touches exactly that many in every one of them. `tile_source`: 0 in slots at or past the device's count. `tile_vals`: Nonnegative; slots at or past the device's count hold stale values that are not part of A.
All inputs are finite; a program needn't handle non-finite values.
Results may differ from the reference program's by a relative error of at most 0.0047.
Values may be sent and summed in bfloat16 or wider, within the bound.
No kernel may reach another device: no remote copies, remote signals or barrier semaphores. Data moves between devices by JAX's collectives and lax.ppermute only.
A program may use at most 128 MiB of HBM per device.

```python
import jax
import jax.numpy as jnp
from jax import lax

F = 128
HID = 256
TILE = 128
TPD = 16
SLOTS = 256
NODES = 524288
N_ROW = 16
N_COL = 16


def shared_counts(key):
    key = jax.random.fold_in(key, 101)
    first_key, second_key = jax.random.split(key, 2)
    draws = jax.random.randint(first_key, (N_ROW, N_COL), 1, 1025)
    lowest = SLOTS // 8
    counts = lowest + (SLOTS - lowest) * (draws * draws // 1024) // 1024
    chosen = jax.random.randint(second_key, (), 0, N_ROW * N_COL)
    flat_counts = jnp.where(jnp.arange(N_ROW * N_COL) == chosen, SLOTS, counts.reshape(-1))
    return flat_counts.reshape(N_ROW, N_COL).astype(jnp.int32)


def live_slots(key):
    counts = shared_counts(key)
    return jnp.arange(SLOTS)[None, None, :] < counts[:, :, None]


def draw_tile_count(key, part):
    return shared_counts(key)


def draw_tile_dest(key, part):
    is_live = live_slots(key)
    key = jax.random.fold_in(key, 3)
    score_key, col_key, pick_key = jax.random.split(key, 3)
    half = TPD // 2
    scores = jax.random.randint(score_key, (N_ROW, N_COL, N_COL, TPD), 0, 1 << 20) * TPD + jnp.arange(TPD, dtype=jnp.int32)
    allowed = jnp.argsort(scores, axis=-1)[..., :half].reshape(N_ROW, N_COL, N_COL * half)
    slot = jnp.arange(SLOTS, dtype=jnp.int32)[None, None, :]
    covering = slot < N_COL * half
    random_cols = jax.random.randint(col_key, (N_ROW, N_COL, SLOTS), 0, N_COL)
    random_picks = jax.random.randint(pick_key, (N_ROW, N_COL, SLOTS), 0, half)
    cols = jnp.where(covering, slot // half, random_cols)
    picks = jnp.where(covering, slot % half, random_picks)
    inner = jnp.take_along_axis(allowed, (cols * half + picks).astype(jnp.int32), axis=-1)
    ids = cols * TPD + inner
    return jnp.where(is_live, ids, 0).astype(jnp.int32)


def draw_tile_source(key, part):
    is_live = live_slots(key)
    key = jax.random.fold_in(key, 5)
    ids = jax.random.randint(key, (N_ROW, N_COL, SLOTS), 0, N_ROW * TPD)
    return jnp.where(is_live, ids, 0).astype(jnp.int32)


def draw_tile_vals(key, part):
    key = jax.random.fold_in(key, 7)
    scale = (7.0 * TPD / (SLOTS * TILE)) ** 0.5
    shape = (N_ROW, N_COL, SLOTS, TILE, TILE)
    values = jax.random.uniform(key, shape, jnp.float32) * scale
    return values.astype(jnp.bfloat16)


def block_levels(rng, dims, cuts, low, high):
    factor_of = 1.0
    for position, blocks in cuts:
        heights = jax.random.uniform(jax.random.fold_in(jax.random.fold_in(rng, 6), position), (blocks,), jnp.float32, low / len(cuts), high / len(cuts))
        factor_of = factor_of * jnp.repeat(jnp.exp(heights), dims[position] // blocks).reshape((-1,) + (1,) * (len(dims) - 1 - position))
    return factor_of


def normal_values(stream_key, dims, scale, limit, cuts=(), kind=jnp.bfloat16):
    entries = scale * jax.random.normal(stream_key, dims, jnp.float32)
    if cuts:
        entries = entries * block_levels(stream_key, dims, cuts, -0.22, 0.18)
    return jnp.clip(entries, -limit, limit).astype(kind)


def setup_inputs(seed: int = 0) -> dict:
    seeds = jax.random.split(jax.random.key(seed), 8)
    node_feats = normal_values(seeds[0], (NODES, F), 1.0, 6.0, ((0, 256),))
    tile_vals = draw_tile_vals(jax.random.fold_in(seeds[7], 71), 0)
    tile_dest = draw_tile_dest(jax.random.fold_in(seeds[7], 71), 0)
    tile_source = draw_tile_source(jax.random.fold_in(seeds[7], 71), 0)
    tile_count = draw_tile_count(jax.random.fold_in(seeds[7], 71), 0)
    weight = normal_values(seeds[5], (F, HID), F ** -0.5, 0.5)
    out_bias = normal_values(seeds[6], (HID,), 0.5, 3.0, (), jnp.float32)
    return {"node_feats": node_feats, "tile_vals": tile_vals, "tile_dest": tile_dest, "tile_source": tile_source, "tile_count": tile_count, "weight": weight, "out_bias": out_bias}


def reference(node_feats, tile_vals, tile_dest, tile_source, tile_count, weight, out_bias):
    tile_size = tile_vals.shape[-1]
    feat_width = node_feats.shape[1]
    slot_count = tile_vals.shape[2]
    grid = node_feats.reshape(N_ROW, N_COL, -1, tile_size, feat_width)

    def row_total(row_index):
        def add_device(col_index, acc):
            source = lax.dynamic_index_in_dim(grid, col_index, 1, keepdims=False).reshape(-1, tile_size, feat_width)
            row_tiles = lax.dynamic_index_in_dim(tile_vals, row_index, 0, keepdims=False)
            tile_set = lax.dynamic_index_in_dim(row_tiles, col_index, 0, keepdims=False)
            row_dest = lax.dynamic_index_in_dim(tile_dest, row_index, 0, keepdims=False)
            dest_ids = lax.dynamic_index_in_dim(row_dest, col_index, 0, keepdims=False)
            row_src = lax.dynamic_index_in_dim(tile_source, row_index, 0, keepdims=False)
            source_ids = lax.dynamic_index_in_dim(row_src, col_index, 0, keepdims=False)
            row_counts = lax.dynamic_index_in_dim(tile_count, row_index, 0, keepdims=False)
            live_count = lax.dynamic_index_in_dim(row_counts, col_index, 0, keepdims=False)
            is_live = jnp.arange(slot_count, dtype=jnp.int32) < live_count
            products = jnp.einsum("kij,kjf->kif", tile_set.astype(jnp.float32), source[source_ids].astype(jnp.float32))
            products = jnp.where(is_live[:, None, None], products, jnp.zeros_like(products))
            return acc.at[dest_ids].add(products)

        start_acc = jnp.zeros((N_COL * TPD, tile_size, feat_width), jnp.float32)
        return lax.fori_loop(0, N_COL, add_device, start_acc)

    aggregated = lax.map(row_total, jnp.arange(N_ROW, dtype=jnp.int32)).reshape(-1, feat_width)
    hidden = jnp.dot(aggregated.astype(jnp.bfloat16), weight, preferred_element_type=jnp.float32) + out_bias
    return jnp.maximum(hidden, 0.0).astype(jnp.bfloat16)
```

```python
import functools

import jax
import jax.numpy as jnp
from jax import lax
from jax.experimental import pallas as pl
from jax.experimental.pallas import tpu as pltpu
from jax.sharding import PartitionSpec as P

TILE = 128
TPD = 16
SLOTS = 256
NY, NXLO, NCORE = 4, 2, 2
NZ, NXHI = 8, 2
ROWS = TPD * TILE
HALF_SLOTS = 8
OWN_BLOCKS = NZ * TPD
OTHER_BLOCKS = NZ * HALF_SLOTS
TRASH = OWN_BLOCKS
GROUP = 8
LIST = SLOTS + GROUP
MAP_AT = 2 * LIST
COUNT_AT = MAP_AT + OTHER_BLOCKS
PLAN = 640
THIRDS = (688, 688, 672)
LOAD = 32

VMEM = pltpu.VMEM
SMEM_SPEC = pl.BlockSpec(memory_space=pltpu.SMEM)
VMEM_SPEC = pl.BlockSpec(memory_space=pltpu.VMEM)
ANY_SPEC = pl.BlockSpec(memory_space=pl.ANY)


def row_perm(change):
    pairs = []
    for y in range(NY):
        for x in range(NXLO):
            for k in range(NCORE):
                ty, tx, tk = change(y, x, k)
                pairs.append(((y * NXLO + x) * NCORE + k, (ty % NY * NXLO + tx) * NCORE + tk))
    return pairs


FROM_UP = row_perm(lambda y, x, k: (y - 1, x, k))
FROM_DOWN = row_perm(lambda y, x, k: (y + 1, x, k))
FROM_SIDE = row_perm(lambda y, x, k: (y, 1 - x, k))
FROM_CORE = row_perm(lambda y, x, k: (y, x, 1 - k))
Z_PLUS = [(z * NXHI + x, (z + 1) % NZ * NXHI + x) for z in range(NZ) for x in range(NXHI)]
Z_MINUS = [(z * NXHI + x, (z - 1) % NZ * NXHI + x) for z in range(NZ) for x in range(NXHI)]
X_FLIP = [(z * NXHI + x, z * NXHI + 1 - x) for z in range(NZ) for x in range(NXHI)]


def plan_kernel(place, dest, source, partner_dest, plan, slot_of, used):
    my_y, my_x, my_k, my_z, my_xhi = (place[i] for i in range(5))

    def clear(i, _):
        slot_of[i] = -1
        return 0

    def clear_lists(i, _):
        plan[i] = TRASH << 16
        return 0

    lax.fori_loop(0, SLOTS, clear, 0, unroll=8)
    lax.fori_loop(0, MAP_AT, clear_lists, 0, unroll=8)

    def clear_map(i, _):
        plan[MAP_AT + i] = TPD
        return 0

    lax.fori_loop(0, OTHER_BLOCKS, clear_map, 0, unroll=8)
    for i in range(2 * NZ):
        used[i] = 0

    def slot_for(block, away, at):
        held = slot_of[block]
        is_new = held < 0
        count = used[at + away]
        slot = jnp.where(is_new, count, held)
        slot_of[block] = slot
        used[at + away] = count + is_new.astype(jnp.int32)
        return slot

    def split(block):
        col = block // TPD
        away = (col // NXHI - my_z + NZ) % NZ
        return away, col % NXHI, block % TPD

    def place_tile(i, carry):
        block = dest[i]
        s = source[i]
        row = s // TPD
        rel_y = (row // (NXLO * NCORE) - my_y + NY) % NY
        rel_x = (row // NCORE % NXLO - my_x + NXLO) % NXLO
        rel_k = (row % NCORE - my_k + NCORE) % NCORE
        rel = ((rel_y * NXLO + rel_x) * NCORE + rel_k) * TPD + s % TPD
        away, half, inner = split(jnp.maximum(block, 0))

        def other(c):
            slot = slot_for(block, away, 0)
            plan[c[0]] = i | (rel << 8) | ((away * HALF_SLOTS + slot) << 16)
            return c[0] + 1, c[1]

        def own(c):
            plan[LIST + c[1]] = i | (rel << 8) | ((away * TPD + inner) << 16)
            return c[0], c[1] + 1

        def live(c):
            return lax.cond(half == my_xhi, own, other, c)

        return lax.cond(block >= 0, live, lambda c: c, carry)

    n_other, n_own = lax.fori_loop(0, SLOTS, place_tile, (jnp.int32(0), jnp.int32(0)))

    def place_partner(i, _):
        block = partner_dest[i]
        away, half, inner = split(jnp.maximum(block, 0))

        @pl.when((block >= 0) & (half == my_xhi))
        def _():
            slot = slot_for(block, away, NZ)
            plan[MAP_AT + away * HALF_SLOTS + slot] = inner

        return 0

    lax.fori_loop(0, SLOTS, place_partner, 0)
    plan[COUNT_AT] = (n_other + GROUP - 1) // GROUP
    plan[COUNT_AT + 1] = (n_own + GROUP - 1) // GROUP
    plan[COUNT_AT + 2] = n_other + n_own


def make_plan(place, dest, source, partner_dest):
    return pl.pallas_call(
        plan_kernel,
        out_shape=jax.ShapeDtypeStruct((PLAN,), jnp.int32),
        in_specs=[SMEM_SPEC] * 4,
        out_specs=SMEM_SPEC,
        scratch_shapes=[pltpu.SMEM((SLOTS,), jnp.int32), pltpu.SMEM((2 * NZ,), jnp.int32)],
        name="plan",
    )(place, dest, source, partner_dest)


def add_products(plan, first, groups, tiles, feats, acc):
    def one_group(g, _):
        entries = [plan[first + g * GROUP + i] for i in range(GROUP)]
        products = [
            jnp.dot(
                tiles[e & 255],
                feats[pl.ds(pl.multiple_of(((e >> 8) & 255) * TILE, TILE), TILE), :],
                preferred_element_type=jnp.float32,
            )
            for e in entries
        ]
        for e, product in zip(entries, products):
            acc[e >> 16] += product
        return 0

    lax.fori_loop(0, groups, one_group, 0)


def other_kernel(pieces, plan, *refs):
    tiles_hbm = refs[0]
    feats_hbm = refs[1 : 1 + len(pieces)]
    refs = refs[1 + len(pieces) :]
    sends, (tiles, feats, acc, sems) = refs[:NZ], refs[NZ:]
    feat_copies = [
        pltpu.make_async_copy(src, feats.at[pl.ds(at, n), :], sems.at[0])
        for src, (at, n) in zip(feats_hbm, pieces)
    ]
    for copy in feat_copies:
        copy.start()

    def tile_copy(j):
        at = pl.ds(j * LOAD, LOAD)
        return pltpu.make_async_copy(tiles_hbm.at[at], tiles.at[at], sems.at[1])

    for j in range(SLOTS // LOAD):
        tile_copy(j).start()

    def clear(i, _):
        acc[i] = jnp.zeros((TILE, acc.shape[2]), jnp.float32)
        return 0

    lax.fori_loop(0, OTHER_BLOCKS, clear, 0, unroll=4)
    for j in range(SLOTS // LOAD):
        tile_copy(j).wait()
    for copy in feat_copies:
        copy.wait()
    add_products(plan, 0, plan[COUNT_AT], tiles, feats, acc)
    for away, send in enumerate(sends):
        send[...] = acc[pl.ds(away * HALF_SLOTS, HALF_SLOTS)].astype(send.dtype)


def own_kernel(plan, tiles, feats, *refs):
    chunks, acc = refs[:NZ], refs[NZ]

    def clear(i, _):
        acc[i] = jnp.zeros((TILE, acc.shape[2]), jnp.float32)
        return 0

    lax.fori_loop(0, OWN_BLOCKS, clear, 0, unroll=4)
    add_products(plan, LIST, plan[COUNT_AT + 1], tiles, feats, acc)
    for away, chunk in enumerate(chunks):
        chunk[...] = acc[pl.ds(away * TPD, TPD)]


def gather_compute(plan, tile_set, pieces, arrays, width):
    bf = jnp.bfloat16
    block = lambda n, dtype: jax.ShapeDtypeStruct((n, TILE, width), dtype)
    outs = pl.pallas_call(
        functools.partial(other_kernel, pieces),
        out_shape=[block(HALF_SLOTS, bf)] * NZ
        + [VMEM((SLOTS, TILE, TILE), bf), VMEM((SLOTS * TILE, width), bf)],
        in_specs=[SMEM_SPEC] + [ANY_SPEC] * (1 + len(arrays)),
        out_specs=[VMEM_SPEC] * (NZ + 2),
        scratch_shapes=[
            VMEM((TRASH + 1, TILE, width), jnp.float32),
            pltpu.SemaphoreType.DMA((2,)),
        ],
        compiler_params=pltpu.CompilerParams(vmem_limit_bytes=40 << 20),
        name="other_half",
    )(plan, tile_set, *arrays)
    sends, tiles, feats = outs[:NZ], outs[NZ], outs[NZ + 1]
    tiles = pltpu.with_memory_space_constraint(tiles, pltpu.VMEM)
    feats = pltpu.with_memory_space_constraint(feats, pltpu.VMEM)

    def own_part():
        return pl.pallas_call(
            own_kernel,
            out_shape=[block(TPD, jnp.float32)] * NZ,
            in_specs=[SMEM_SPEC, VMEM_SPEC, VMEM_SPEC],
            out_specs=[VMEM_SPEC] * NZ,
            scratch_shapes=[VMEM((TRASH + 1, TILE, width), jnp.float32)],
            compiler_params=pltpu.CompilerParams(vmem_limit_bytes=40 << 20),
            name="own_half",
        )(plan, tiles, feats)

    return sends, own_part


def merge(away, plan, own, arrived, passed, acc):
    acc[pl.ds(0, TPD)] = own[...]
    for ref, at in passed:
        n = ref.shape[0]
        acc[pl.ds(at, n)] += ref[...].astype(jnp.float32)
    for i in range(HALF_SLOTS):
        acc[plan[MAP_AT + away * HALF_SLOTS + i]] += arrived[i].astype(jnp.float32)


def hop_kernel(away, pass_at, cuts, plan, own, arrived, *refs):
    passed = list(zip(refs[: len(pass_at)], pass_at))
    outs, acc = refs[len(pass_at) : -1], refs[-1]
    merge(away, plan, own, arrived, passed, acc)
    for out, (at, n) in zip(outs, cuts):
        out[...] = acc[pl.ds(at, n)].astype(out.dtype)


def hop(away, plan, own, arrived, passed, pass_at, cuts):
    width = own.shape[-1]
    out = pl.pallas_call(
        functools.partial(hop_kernel, away, pass_at, cuts),
        out_shape=[jax.ShapeDtypeStruct((n, TILE, width), jnp.bfloat16) for _, n in cuts],
        in_specs=[SMEM_SPEC] + [VMEM_SPEC] * (2 + len(passed)),
        out_specs=[VMEM_SPEC] * len(cuts),
        scratch_shapes=[VMEM((TPD + 1, TILE, width), jnp.float32)],
        name=f"hop_{away}",
    )(plan, own, arrived, *passed)
    return out


def last_kernel(plan, own, arrived, passed_a, passed_b, weight, bias, out, acc):
    merge(0, plan, own, arrived, [(passed_a, 0), (passed_b, 0)], acc)
    total = acc[pl.ds(0, TPD)].reshape(ROWS, -1).astype(jnp.bfloat16)
    hidden = jnp.dot(total, weight[...], preferred_element_type=jnp.float32) + bias[...]
    out[...] = jnp.maximum(hidden, 0.0).astype(out.dtype)


def last(plan, own, arrived, passed_a, passed_b, weight, bias):
    return pl.pallas_call(
        last_kernel,
        out_shape=jax.ShapeDtypeStruct((ROWS, weight.shape[1]), jnp.bfloat16),
        in_specs=[SMEM_SPEC] + [VMEM_SPEC] * 6,
        out_specs=VMEM_SPEC,
        scratch_shapes=[VMEM((TPD + 1, TILE, own.shape[-1]), jnp.float32)],
        name="last",
    )(plan, own, arrived, passed_a, passed_b, weight, bias)


def gather(mine):
    send = lambda array, perm: lax.ppermute(array, "row", perm)
    got = [(0, 0, 0, ROWS, mine)]
    up, down, side = send(mine, FROM_UP), send(mine, FROM_DOWN), send(mine, FROM_SIDE)
    got += [(1, 0, 0, ROWS, up), (3, 0, 0, ROWS, down), (0, 1, 0, ROWS, side)]
    far = send(up, FROM_UP)
    down_side = send(side, FROM_DOWN)
    up_side = send(up, FROM_SIDE)
    got += [(2, 0, 0, ROWS, far), (3, 1, 0, ROWS, down_side), (1, 1, 0, ROWS, up_side)]
    at = 0
    for n, array, perm in zip(
        THIRDS, (up_side, down_side, far), (FROM_UP, FROM_DOWN, FROM_SIDE)
    ):
        got.append((2, 1, at, n, send(array[at : at + n], perm)))
        at += n
    pieces, arrays = [], []
    for y, x, first, n, array in got:
        for k in range(NCORE):
            pieces.append((((y * NXLO + x) * NCORE + k) * ROWS + first, n))
            arrays.append(array if k == 0 else send(array, FROM_CORE))
    return tuple(pieces), arrays


def on_device(node_feats, tile_vals, tile_dest, tile_source, tile_count, weight, out_bias):
    row, col = lax.axis_index("row"), lax.axis_index("col")
    place = jnp.stack(
        [row // (NXLO * NCORE), row // NCORE % NXLO, row % NCORE, col // NXHI, col % NXHI]
    ).astype(jnp.int32)
    slots = jnp.arange(SLOTS, dtype=jnp.int32)
    dest = jnp.where(slots < tile_count[0, 0], tile_dest[0, 0], -1)
    partner_dest = lax.ppermute(dest, "col", X_FLIP)
    pieces, arrays = gather(node_feats)
    plan = make_plan(place, dest, tile_source[0, 0], partner_dest)
    sends, own_part = gather_compute(plan, tile_vals[0, 0], pieces, arrays, node_feats.shape[1])
    order = (4, 3, 5, 2, 6, 1, 7, 0)
    arrived = {}
    for away in order:
        arrived[away] = lax.ppermute(sends[away], "col", X_FLIP)
    own = own_part()
    half = TPD // 2
    plus, minus = hop(
        4, plan, own[4], arrived[4], (), (), ((0, half), (half, half))
    )
    plus, minus = lax.ppermute(plus, "col", Z_PLUS), lax.ppermute(minus, "col", Z_MINUS)
    for step, (a, b) in enumerate(((3, 5), (2, 6), (1, 7))):
        at_a, at_b = ((0,), (half,)) if step == 0 else ((0,), (0,))
        (plus,) = hop(a, plan, own[a], arrived[a], (plus,), at_a, ((0, TPD),))
        plus = lax.ppermute(plus, "col", Z_PLUS)
        (minus,) = hop(b, plan, own[b], arrived[b], (minus,), at_b, ((0, TPD),))
        minus = lax.ppermute(minus, "col", Z_MINUS)
    return last(plan, own[0], arrived[0], plus, minus, weight, out_bias.reshape(1, -1))


def solution(mesh):
    return jax.shard_map(
        on_device,
        mesh=mesh,
        in_specs=(
            P(("row", "col"), None),
            P("row", "col", None, None, None),
            P("row", "col", None),
            P("row", "col", None),
            P("row", "col"),
            P(),
            P(),
        ),
        out_specs=P(("row", "col"), None),
        check_vma=False,
    )
```

```python
import functools

import jax
import jax.numpy as jnp
from jax import lax
from jax.experimental import pallas as pl
from jax.experimental.pallas import tpu as pltpu
from jax.sharding import PartitionSpec as P

TILE = 128
TPD = 16
SLOTS = 256
NY, NXLO, NCORE = 4, 2, 2
NZ, NXHI = 8, 2
ROWS = TPD * TILE
HALF_SLOTS = 8
OWN_BLOCKS = NZ * TPD
OTHER_BLOCKS = NZ * HALF_SLOTS
TRASH = OWN_BLOCKS
GROUP = 8
WIDTH = 384
THIRDS = (688, 688, 672)

VMEM = pltpu.VMEM
SMEM_SPEC = pl.BlockSpec(memory_space=pltpu.SMEM)
VMEM_SPEC = pl.BlockSpec(memory_space=pltpu.VMEM)
ANY_SPEC = pl.BlockSpec(memory_space=pl.ANY)


def row_perm(change):
    pairs = []
    for y in range(NY):
        for x in range(NXLO):
            for k in range(NCORE):
                ty, tx, tk = change(y, x, k)
                pairs.append(((y * NXLO + x) * NCORE + k, (ty % NY * NXLO + tx) * NCORE + tk))
    return pairs


FROM_UP = row_perm(lambda y, x, k: (y - 1, x, k))
FROM_DOWN = row_perm(lambda y, x, k: (y + 1, x, k))
FROM_SIDE = row_perm(lambda y, x, k: (y, 1 - x, k))
FROM_CORE = row_perm(lambda y, x, k: (y, x, 1 - k))
Z_PLUS = [(z * NXHI + x, (z + 1) % NZ * NXHI + x) for z in range(NZ) for x in range(NXHI)]
Z_MINUS = [(z * NXHI + x, (z - 1) % NZ * NXHI + x) for z in range(NZ) for x in range(NXHI)]
X_FLIP = [(z * NXHI + x, z * NXHI + 1 - x) for z in range(NZ) for x in range(NXHI)]


def call(kernel, name, **kwargs):
    return pl.pallas_call(
        kernel,
        name=name,
        cost_estimate=pl.CostEstimate(flops=0, bytes_accessed=0, transcendentals=0),
        compiler_params=pltpu.CompilerParams(vmem_limit_bytes=16 << 20),
        **kwargs,
    )


def keep(array):
    return pltpu.with_memory_space_constraint(array, pltpu.VMEM)


def iota(shape, dim):
    return lax.broadcasted_iota(jnp.int32, shape, dim)


def to_column(row):
    n = row.shape[1]
    square = jnp.broadcast_to(row, (n, n))
    return jnp.sum(jnp.where(iota((n, n), 0) == iota((n, n), 1), square, 0.0), 1, keepdims=True)


def to_row(column):
    n = column.shape[0]
    square = jnp.broadcast_to(column, (n, n))
    return jnp.sum(jnp.where(iota((n, n), 0) == iota((n, n), 1), square, 0.0), 0, keepdims=True)


def split_dest(block, my_z):
    block = jnp.maximum(block, 0)
    away = ((block // (NXHI * TPD)) - my_z) & (NZ - 1)
    return away, (block // TPD) & (NXHI - 1), block & (TPD - 1)


def slots_of(key, chosen):
    hit = (iota((OWN_BLOCKS, SLOTS), 0) == key) & chosen
    touched = jnp.max(jnp.where(hit, 1.0, 0.0), axis=1, keepdims=True)
    a, b = iota((OWN_BLOCKS, OWN_BLOCKS), 0), iota((OWN_BLOCKS, OWN_BLOCKS), 1)
    before = (b < a) & (b // TPD == a // TPD)
    rank = jnp.sum(jnp.where(before, to_row(touched), 0.0), axis=1, keepdims=True)
    return hit, touched, rank


def listed(chosen, value):
    mark = to_column(jnp.where(chosen, 1.0, 0.0))
    earlier = iota((SLOTS, SLOTS), 0) < iota((SLOTS, SLOTS), 1)
    at = to_column(jnp.sum(jnp.where(earlier, mark, 0.0), axis=0, keepdims=True))
    count = jnp.sum(mark)
    place = iota((SLOTS, WIDTH), 1).astype(jnp.float32)
    value = to_column(value.astype(jnp.float32))
    row = jnp.sum(jnp.where((at == place) & (mark > 0), value, 0.0), axis=0, keepdims=True)
    empty = iota((1, WIDTH), 1).astype(jnp.float32) >= count
    return jnp.where(empty, float(TRASH << 16), row).astype(jnp.int32), count


def plan_kernel(where, dest, source, partner_dest, plan):
    my_y, my_x, my_k, my_z, my_xhi = (where[i] for i in range(5))
    block, from_block = dest[...], source[...]
    row = from_block // TPD
    rel = ((row // (NXLO * NCORE)) - my_y) & (NY - 1)
    rel = rel * NXLO + (((row // NCORE) - my_x) & (NXLO - 1))
    rel = rel * NCORE + ((row - my_k) & (NCORE - 1))
    rel = rel * TPD + (from_block & (TPD - 1))
    away, half, inner = split_dest(block, my_z)
    key = away * TPD + inner
    is_own = (block >= 0) & (half == my_xhi)
    is_other = (block >= 0) & (half != my_xhi)
    tile = iota((1, SLOTS), 1) + rel * 256
    hit, _, rank = slots_of(key, is_other)
    slot = jnp.sum(jnp.where(hit, rank, 0.0), axis=0, keepdims=True).astype(jnp.int32)
    other, n_other = listed(is_other, tile + (away * HALF_SLOTS + slot) * 65536)
    own, n_own = listed(is_own, tile + key * 65536)
    away, half, inner = split_dest(partner_dest[...], my_z)
    sent = (partner_dest[...] >= 0) & (half == my_xhi)
    _, touched, rank = slots_of(away * TPD + inner, sent)
    slot = to_row(jnp.where(touched > 0, rank, float(HALF_SLOTS))).astype(jnp.int32)
    plan[0:1, :] = other
    plan[1:2, :] = own
    plan[2:3, 0:OWN_BLOCKS] = slot
    lane = iota((1, WIDTH - OWN_BLOCKS), 1)
    counts = jnp.where(lane == 0, n_other, n_own).astype(jnp.int32)
    plan[2:3, OWN_BLOCKS:] = (counts + (GROUP - 1)) // GROUP


def make_plan(where, dest, source, partner_dest):
    return call(
        plan_kernel,
        "plan",
        out_shape=jax.ShapeDtypeStruct((8, WIDTH), jnp.int32),
        in_specs=[SMEM_SPEC] + [VMEM_SPEC] * 3,
        out_specs=VMEM_SPEC,
    )(where, dest, source, partner_dest)


def add_products(plan, which, tiles, feats, acc):
    def one_group(g, _):
        entries = [plan[which, g * GROUP + i] for i in range(GROUP)]
        products = [
            jnp.dot(
                tiles[e & 255],
                feats[pl.ds(pl.multiple_of(((e >> 8) & 255) * TILE, TILE), TILE), :],
                preferred_element_type=jnp.float32,
            )
            for e in entries
        ]
        for e, product in zip(entries, products):
            acc[e >> 16] += product
        return 0

    lax.fori_loop(0, plan[2, OWN_BLOCKS + which], one_group, 0)


def clear_blocks(acc, n):
    def clear(i, _):
        acc[i] = jnp.zeros(acc.shape[1:], acc.dtype)
        return 0

    lax.fori_loop(0, n, clear, 0, unroll=4)


def load_tiles_kernel(tiles_hbm, tiles, sem):
    copy = pltpu.make_async_copy(tiles_hbm, tiles, sem)
    copy.start()
    copy.wait()


def load_tiles(tile_set):
    return call(
        load_tiles_kernel,
        "load_tiles",
        out_shape=VMEM(tile_set.shape, tile_set.dtype),
        in_specs=[ANY_SPEC],
        out_specs=VMEM_SPEC,
        scratch_shapes=[pltpu.SemaphoreType.DMA(())],
    )(tile_set)


def load_feats_kernel(pieces, has_base, *refs):
    feats = refs[-1]
    for (at, n), ref in zip(pieces, refs[has_base:]):
        feats[pl.ds(at, n), :] = ref[...]


def load_feats(base, pieces):
    places = tuple((at, array.shape[0]) for at, array in pieces)
    arrays = [array for _, array in pieces]
    has_base = base is not None
    return call(
        functools.partial(load_feats_kernel, places, has_base),
        "load_feats",
        out_shape=VMEM((SLOTS * TILE, arrays[0].shape[1]), arrays[0].dtype),
        in_specs=[VMEM_SPEC] * (has_base + len(arrays)),
        out_specs=VMEM_SPEC,
        input_output_aliases={0: 0} if has_base else {},
    )(*([keep(base)] if has_base else []), *arrays)


def other_kernel(plan, tiles, feats, *refs):
    sends, acc = refs[:NZ], refs[NZ]
    clear_blocks(acc, OTHER_BLOCKS)
    add_products(plan, 0, tiles, feats, acc)
    for away, send in enumerate(sends):
        send[...] = acc[pl.ds(away * HALF_SLOTS, HALF_SLOTS)].astype(send.dtype)


def other_half(plan, tiles, feats):
    width = feats.shape[1]
    return call(
        other_kernel,
        "other_half",
        out_shape=[VMEM((HALF_SLOTS, TILE, width), jnp.bfloat16)] * NZ,
        in_specs=[SMEM_SPEC, VMEM_SPEC, VMEM_SPEC],
        out_specs=[VMEM_SPEC] * NZ,
        scratch_shapes=[VMEM((TRASH + 1, TILE, width), jnp.float32)],
    )(plan, keep(tiles), keep(feats))


def own_kernel(plan, tiles, feats, acc):
    clear_blocks(acc, OWN_BLOCKS)
    add_products(plan, 1, tiles, feats, acc)


def own_half(plan, tiles, feats):
    return call(
        own_kernel,
        "own_half",
        out_shape=VMEM((TRASH + 1, TILE, feats.shape[1]), jnp.float32),
        in_specs=[SMEM_SPEC, VMEM_SPEC, VMEM_SPEC],
        out_specs=VMEM_SPEC,
    )(plan, keep(tiles), keep(feats))


def merged(away, plan, own, arrived, passed, i):
    total = own[away * TPD + i]
    for ref, at in passed:
        if at <= i < at + ref.shape[0]:
            total += ref[i - at].astype(jnp.float32)
    slot = plan[2, away * TPD + i]
    seen = (slot < HALF_SLOTS).astype(jnp.float32)
    return total + arrived[jnp.minimum(slot, HALF_SLOTS - 1)].astype(jnp.float32) * seen


def hop_kernel(away, pass_at, cuts, plan, own, arrived, *refs):
    passed = list(zip(refs[: len(pass_at)], pass_at))
    for out, (at, n) in zip(refs[len(pass_at) :], cuts):
        for i in range(n):
            out[i] = merged(away, plan, own, arrived, passed, at + i).astype(out.dtype)


def hop(away, plan, own, arrived, passed, pass_at, cuts):
    width = own.shape[-1]
    return call(
        functools.partial(hop_kernel, away, pass_at, cuts),
        f"hop_{away}",
        out_shape=[VMEM((n, TILE, width), jnp.bfloat16) for _, n in cuts],
        in_specs=[SMEM_SPEC] + [VMEM_SPEC] * (2 + len(passed)),
        out_specs=[VMEM_SPEC] * len(cuts),
    )(plan, keep(own), arrived, *passed)


def last_kernel(plan, own, arrived, passed_a, passed_b, weight, bias, out):
    passed = [(passed_a, 0), (passed_b, 0)]
    for i in range(TPD):
        total = merged(0, plan, own, arrived, passed, i).astype(jnp.bfloat16)
        hidden = jnp.dot(total, weight[...], preferred_element_type=jnp.float32) + bias[...]
        out[pl.ds(i * TILE, TILE), :] = jnp.maximum(hidden, 0.0).astype(out.dtype)


def last(plan, own, arrived, passed_a, passed_b, weight, bias):
    return call(
        last_kernel,
        "last",
        out_shape=jax.ShapeDtypeStruct((ROWS, weight.shape[1]), jnp.bfloat16),
        in_specs=[SMEM_SPEC] + [VMEM_SPEC] * 6,
        out_specs=VMEM_SPEC,
    )(plan, keep(own), arrived, passed_a, passed_b, weight, bias)


def send(array, perm):
    return lax.ppermute(array, "row", perm)


def both_cores(y, x, array, first=0):
    at = ((y * NXLO + x) * NCORE) * ROWS + first
    return [(at, array), (at + ROWS, send(array, FROM_CORE))]


def on_device(node_feats, tile_vals, tile_dest, tile_source, tile_count, weight, out_bias):
    row, col = lax.axis_index("row"), lax.axis_index("col")
    where = jnp.stack(
        [row // (NXLO * NCORE), row // NCORE % NXLO, row % NCORE, col // NXHI, col % NXHI]
    ).astype(jnp.int32)
    slots = jnp.arange(SLOTS, dtype=jnp.int32)[None, :]
    dest = jnp.where(slots < tile_count[0, 0], tile_dest[0], -1)
    partner_dest = lax.ppermute(dest, "col", X_FLIP)
    up, down, side = (send(node_feats, p) for p in (FROM_UP, FROM_DOWN, FROM_SIDE))
    own_pieces = both_cores(0, 0, node_feats)
    plan = make_plan(where, dest, tile_source[0], partner_dest)
    tiles = load_tiles(tile_vals[0, 0])
    up, down, side, plan = lax.optimization_barrier((up, down, side, plan))
    far, down_side, up_side = send(up, FROM_UP), send(side, FROM_DOWN), send(up, FROM_SIDE)
    pieces = both_cores(1, 0, up) + both_cores(3, 0, down) + both_cores(0, 1, side)
    feats = load_feats(None, own_pieces + pieces)
    far, down_side, up_side, tiles, feats = lax.optimization_barrier(
        (far, down_side, up_side, tiles, feats)
    )
    thirds, at = [], 0
    for n, array, perm in zip(
        THIRDS, (up_side, down_side, far), (FROM_UP, FROM_DOWN, FROM_SIDE)
    ):
        thirds.append(send(array[at : at + n], perm))
        at += n
    feats = load_feats(
        feats, both_cores(2, 0, far) + both_cores(3, 1, down_side) + both_cores(1, 1, up_side)
    )
    thirds, feats = lax.optimization_barrier((thirds, feats))
    starts = (0, THIRDS[0], THIRDS[0] + THIRDS[1])
    feats = load_feats(feats, sum((both_cores(2, 1, a, at) for at, a in zip(starts, thirds)), []))
    sends = other_half(plan, tiles, feats)
    arrived = {}
    for away in (4, 3, 5, 2, 6, 1, 7, 0):
        arrived[away] = lax.ppermute(sends[away], "col", X_FLIP)
    own = own_half(plan, tiles, feats)
    half = TPD // 2
    plus, minus = hop(4, plan, own, arrived[4], (), (), ((0, half), (half, half)))
    plus, minus = lax.ppermute(plus, "col", Z_PLUS), lax.ppermute(minus, "col", Z_MINUS)
    for step, (a, b) in enumerate(((3, 5), (2, 6), (1, 7))):
        at_a, at_b = ((0,), (half,)) if step == 0 else ((0,), (0,))
        (plus,) = hop(a, plan, own, arrived[a], (plus,), at_a, ((0, TPD),))
        plus = lax.ppermute(plus, "col", Z_PLUS)
        (minus,) = hop(b, plan, own, arrived[b], (minus,), at_b, ((0, TPD),))
        minus = lax.ppermute(minus, "col", Z_MINUS)
    return last(plan, own, arrived[0], plus, minus, weight, out_bias.reshape(1, -1))


def solution(mesh):
    return jax.shard_map(
        on_device,
        mesh=mesh,
        in_specs=(
            P(("row", "col"), None),
            P("row", "col", None, None, None),
            P("row", "col", None),
            P("row", "col", None),
            P("row", "col"),
            P(),
            P(),
        ),
        out_specs=P(("row", "col"), None),
        check_vma=False,
    )
```

```python
import functools

import jax
import jax.numpy as jnp
from jax import lax
from jax.experimental import pallas as pl
from jax.experimental.pallas import tpu as pltpu
from jax.sharding import PartitionSpec as P

TILE = 128
TPD = 16
SLOTS = 256
NY, NXLO, NCORE = 4, 2, 2
NZ, NXHI = 8, 2
ROWS = TPD * TILE
HALF_SLOTS = 8
OWN_BLOCKS = NZ * TPD
OTHER_BLOCKS = NZ * HALF_SLOTS
GROUP = 16
WIDTH = 512
CLASSES = 5
KINDS = 16
PACKED = ((0, 0), (1, 0), (3, 0), (0, 1), (2, 0), (3, 1), (1, 1), (2, 1))
EARLY = 4
LAST = 7
X_PARTS = ((4,), (3, 5), (2, 6), (1, 7), (0,))
THIRDS = (688, 688, 672)

VMEM = pltpu.VMEM
SMEM_SPEC = pl.BlockSpec(memory_space=pltpu.SMEM)
VMEM_SPEC = pl.BlockSpec(memory_space=pltpu.VMEM)
ANY_SPEC = pl.BlockSpec(memory_space=pl.ANY)


def row_perm(change):
    pairs = []
    for y in range(NY):
        for x in range(NXLO):
            for k in range(NCORE):
                ty, tx, tk = change(y, x, k)
                pairs.append(((y * NXLO + x) * NCORE + k, (ty % NY * NXLO + tx) * NCORE + tk))
    return pairs


FROM_UP = row_perm(lambda y, x, k: (y - 1, x, k))
FROM_DOWN = row_perm(lambda y, x, k: (y + 1, x, k))
FROM_SIDE = row_perm(lambda y, x, k: (y, 1 - x, k))
FROM_CORE = row_perm(lambda y, x, k: (y, x, 1 - k))
Z_PLUS = [(z * NXHI + x, (z + 1) % NZ * NXHI + x) for z in range(NZ) for x in range(NXHI)]
Z_MINUS = [(z * NXHI + x, (z - 1) % NZ * NXHI + x) for z in range(NZ) for x in range(NXHI)]
Z_CHAINS = (Z_PLUS, Z_MINUS)
X_FLIP = [(z * NXHI + x, z * NXHI + 1 - x) for z in range(NZ) for x in range(NXHI)]


def call(kernel, name, **kwargs):
    return pl.pallas_call(
        kernel,
        name=name,
        cost_estimate=pl.CostEstimate(flops=0, bytes_accessed=0, transcendentals=0),
        compiler_params=pltpu.CompilerParams(vmem_limit_bytes=16 << 20),
        **kwargs,
    )


def keep_scalars(array):
    return pltpu.with_memory_space_constraint(array, pltpu.SMEM)


def keep(array):
    return pltpu.with_memory_space_constraint(array, pltpu.VMEM)


def iota(shape, dim):
    return lax.broadcasted_iota(jnp.int32, shape, dim)


def to_column(row):
    n = row.shape[1]
    square = jnp.broadcast_to(row, (n, n))
    return jnp.sum(jnp.where(iota((n, n), 0) == iota((n, n), 1), square, 0.0), 1, keepdims=True)


def to_row(column):
    n = column.shape[0]
    square = jnp.broadcast_to(column, (n, n))
    return jnp.sum(jnp.where(iota((n, n), 0) == iota((n, n), 1), square, 0.0), 0, keepdims=True)


def split_dest(block, my_z):
    block = jnp.maximum(block, 0)
    away = ((block // (NXHI * TPD)) - my_z) & (NZ - 1)
    return away, (block // TPD) & (NXHI - 1), block & (TPD - 1)


def slots_of(key, chosen):
    hit = (iota((OWN_BLOCKS, SLOTS), 0) == key) & chosen
    touched = jnp.max(jnp.where(hit, 1.0, 0.0), axis=1, keepdims=True)
    a, b = iota((OWN_BLOCKS, OWN_BLOCKS), 0), iota((OWN_BLOCKS, OWN_BLOCKS), 1)
    before = (b < a) & (b // TPD == a // TPD)
    rank = jnp.sum(jnp.where(before, to_row(touched), 0.0), axis=1, keepdims=True)
    return hit, touched, rank


def lists_of(kind, value):
    kinds = iota((KINDS, SLOTS), 0)
    n = jnp.sum(jnp.where(kinds == kind, 1, 0).astype(jnp.float32), axis=1, keepdims=True)
    groups = jnp.floor((n + (GROUP - 1)) * (1.0 / GROUP))
    first = jnp.sum(jnp.where(kinds < kind, groups, 0.0), axis=0, keepdims=True) * GROUP
    kind_column = to_column(kind.astype(jnp.float32))
    earlier = iota((SLOTS, SLOTS), 0) < iota((SLOTS, SLOTS), 1)
    same = (kind_column == kind.astype(jnp.float32)) & earlier
    at = first + jnp.sum(jnp.where(same, 1.0, 0.0), axis=0, keepdims=True)
    at = to_column(jnp.where(kind < KINDS, at, -1.0))
    held = at == iota((SLOTS, WIDTH), 1).astype(jnp.float32)
    filled = jnp.sum(jnp.where(held, 1.0, 0.0), axis=0, keepdims=True)
    value = to_column(value.astype(jnp.float32))
    row = jnp.sum(jnp.where(held, value, 0.0), axis=0, keepdims=True).astype(jnp.int32)
    a, b = iota((KINDS, TILE), 0), iota((KINDS, TILE), 1)
    starts = jnp.sum(jnp.where(a < b, groups, 0.0), axis=0, keepdims=True)
    counts = jnp.sum(jnp.where(a == b, groups, 0.0), axis=0, keepdims=True)
    others = jnp.sum(jnp.where(iota((KINDS, 1), 0) < CLASSES, groups, 0.0)) * GROUP
    is_other = iota((1, WIDTH), 1).astype(jnp.float32) < others
    spare = jnp.where(is_other, OTHER_BLOCKS, OWN_BLOCKS) * 65536
    return jnp.where(filled > 0, row, spare), starts.astype(jnp.int32), counts.astype(jnp.int32)


def plan_kernel(where, dest, source, plan):
    my_y, my_x, my_k, my_z, my_xhi = (where[i] for i in range(5))
    block, from_block = dest[...], source[...]
    row = from_block // TPD
    rel = (((row // (NXLO * NCORE)) - my_y) & (NY - 1)) * NXLO
    rel = rel + (((row // NCORE) - my_x) & (NXLO - 1))
    sibling = (row - my_k) & (NCORE - 1)
    slot = jnp.zeros_like(rel)
    for i, (y, x) in enumerate(PACKED):
        slot = jnp.where(rel == y * NXLO + x, i, slot)
    is_far = slot == LAST
    feat = jnp.where(is_far, 0, slot) * TPD + (from_block & (TPD - 1))
    late = jnp.where(slot < EARLY, 0, 1)
    group = jnp.where(is_far, 3 + sibling, jnp.where(sibling == 1, 2, late))
    away, half, inner = split_dest(block, my_z)
    key = away * TPD + inner
    is_own = half == my_xhi
    live = block >= 0
    hit, _, rank = slots_of(key, live & (half != my_xhi))
    slot = jnp.sum(jnp.where(hit, rank, 0.0), axis=0, keepdims=True).astype(jnp.int32)
    to = jnp.where(is_own, key, away * HALF_SLOTS + slot)
    kind = jnp.where(live, jnp.where(is_own, CLASSES, 0) + group, KINDS)
    value = iota((1, SLOTS), 1) + feat * 256 + to * 65536
    row, starts, counts = lists_of(kind, value)
    plan[0:1, :] = row
    plan[1:2, 0:TILE] = starts
    plan[2:3, 0:TILE] = counts


def make_plan(where, dest, source):
    return call(
        plan_kernel,
        "plan",
        out_shape=jax.ShapeDtypeStruct((8, WIDTH), jnp.int32),
        in_specs=[SMEM_SPEC] + [VMEM_SPEC] * 2,
        out_specs=VMEM_SPEC,
    )(where, dest, source)


def map_kernel(where, partner_dest, slots, found, sem):
    my_z, my_xhi = where[3], where[4]
    block = partner_dest[...]
    away, half, inner = split_dest(block, my_z)
    _, touched, rank = slots_of(away * TPD + inner, (block >= 0) & (half == my_xhi))
    slot = to_row(jnp.where(touched > 0, rank, float(HALF_SLOTS)))
    found[...] = slot.astype(jnp.int32)
    copy = pltpu.make_async_copy(found, slots, sem)
    copy.start()
    copy.wait()


def make_map(where, partner_dest):
    return call(
        map_kernel,
        "partner_map",
        out_shape=pltpu.SMEM((1, OWN_BLOCKS), jnp.int32),
        in_specs=[SMEM_SPEC, VMEM_SPEC],
        out_specs=SMEM_SPEC,
        scratch_shapes=[VMEM((1, OWN_BLOCKS), jnp.int32), pltpu.SemaphoreType.DMA(())],
    )(where, partner_dest)


def add_products(plan, kind, tiles, feats, acc):
    def one_group(g, _):
        entries = [plan[0, g * GROUP + i] for i in range(GROUP)]
        products = [
            jnp.dot(
                tiles[e & 255],
                feats[pl.ds(pl.multiple_of(((e >> 8) & 255) * TILE, TILE), TILE), :],
                preferred_element_type=jnp.float32,
            )
            for e in entries
        ]
        for e, product in zip(entries, products):
            acc[e >> 16] += product
        return 0

    first = plan[1, kind]
    lax.fori_loop(first, first + plan[2, kind], one_group, 0)


def clear_blocks(acc, n):
    def clear(i, _):
        acc[i] = jnp.zeros(acc.shape[1:], acc.dtype)
        return 0

    lax.fori_loop(0, n, clear, 0, unroll=4)


def load_tiles_kernel(tiles_hbm, tiles, sem):
    copy = pltpu.make_async_copy(tiles_hbm, tiles, sem)
    copy.start()
    copy.wait()


def load_tiles(tile_set):
    return call(
        load_tiles_kernel,
        "load_tiles",
        out_shape=VMEM(tile_set.shape, tile_set.dtype),
        in_specs=[ANY_SPEC],
        out_specs=VMEM_SPEC,
        scratch_shapes=[pltpu.SemaphoreType.DMA(())],
    )(tile_set)


def pack_kernel(has_base, first, *refs):
    packed = refs[-1]
    for i, ref in enumerate(refs[has_base:-1]):
        packed[pl.ds(first + i * ROWS, ROWS), :] = ref[...]


def pack(base, first, arrays):
    has_base = base is not None
    return call(
        functools.partial(pack_kernel, has_base, first),
        "pack",
        out_shape=VMEM((LAST * ROWS, arrays[0].shape[1]), arrays[0].dtype),
        in_specs=[VMEM_SPEC] * (has_base + len(arrays)),
        out_specs=VMEM_SPEC,
        input_output_aliases={0: 0} if has_base else {},
    )(*([keep(base)] if has_base else []), *arrays)


def join_kernel(*refs):
    at = 0
    for ref in refs[:-1]:
        refs[-1][pl.ds(at, ref.shape[0]), :] = ref[...]
        at += ref.shape[0]


def join(arrays):
    return call(
        join_kernel,
        "join",
        out_shape=VMEM((ROWS, arrays[0].shape[1]), arrays[0].dtype),
        in_specs=[VMEM_SPEC] * len(arrays),
        out_specs=VMEM_SPEC,
    )(*arrays)


def first_kernel(plan, tiles, feats, _, other, own):
    clear_blocks(other, OTHER_BLOCKS)
    clear_blocks(own, OWN_BLOCKS)
    add_products(plan, 0, tiles, feats, other)
    add_products(plan, CLASSES, tiles, feats, own)


def first_products(plan, tiles, feats):
    block = (TILE, feats.shape[1])
    return call(
        first_kernel,
        "first_products",
        out_shape=[
            VMEM(feats.shape, feats.dtype),
            VMEM((OTHER_BLOCKS + 1, *block), jnp.float32),
            VMEM((OWN_BLOCKS + 1, *block), jnp.float32),
        ],
        in_specs=[SMEM_SPEC] + [VMEM_SPEC] * 2,
        out_specs=[VMEM_SPEC] * 3,
        input_output_aliases={2: 0},
    )(plan, keep(tiles), keep(feats))


def more_kernel(kinds, n_feats, plan, tiles, *refs):
    feats, accs = refs[:n_feats], refs[-len(kinds) :]
    for acc, of_acc in zip(accs, kinds):
        for kind, at in of_acc:
            add_products(plan, kind, tiles, feats[at], acc)


def more_products(name, kinds, plan, tiles, feats, accs):
    n = 2 + len(feats)
    return call(
        functools.partial(more_kernel, kinds, len(feats)),
        name,
        out_shape=[VMEM(acc.shape, acc.dtype) for acc in accs],
        in_specs=[SMEM_SPEC] + [VMEM_SPEC] * (n - 1 + len(accs)),
        out_specs=[VMEM_SPEC] * len(accs),
        input_output_aliases={n + i: i for i in range(len(accs))},
    )(plan, keep(tiles), *[keep(f) for f in feats], *[keep(acc) for acc in accs])


def sends_kernel(plan, tiles, far_sibling, _, acc, *sends):
    add_products(plan, 4, tiles, far_sibling, acc)
    for aways, send in zip(X_PARTS, sends):
        for i, away in enumerate(aways):
            blocks = acc[pl.ds(away * HALF_SLOTS, HALF_SLOTS)]
            send[pl.ds(i * HALF_SLOTS, HALF_SLOTS)] = blocks.astype(send.dtype)


def make_sends(plan, tiles, far_sibling, acc):
    return call(
        sends_kernel,
        "make_sends",
        out_shape=[VMEM(acc.shape, acc.dtype)]
        + [VMEM((HALF_SLOTS * len(p), *acc.shape[1:]), jnp.bfloat16) for p in X_PARTS],
        in_specs=[SMEM_SPEC] + [VMEM_SPEC] * 3,
        out_specs=[VMEM_SPEC] * (1 + len(X_PARTS)),
        input_output_aliases={3: 0},
    )(plan, keep(tiles), keep(far_sibling), keep(acc))[1:]


def merged(away, first, slots, own, arrived, passed, i):
    total = own[away * TPD + i]
    for ref, at in passed:
        if at <= i < at + ref.shape[0]:
            total += ref[i - at].astype(jnp.float32)
    slot = slots[0, away * TPD + i]
    seen = (slot < HALF_SLOTS).astype(jnp.float32)
    block = arrived[first + jnp.minimum(slot, HALF_SLOTS - 1)]
    return total + block.astype(jnp.float32) * seen


def hop_kernel(parts, slots, own, arrived, *refs):
    passed, outs = refs[: -len(parts)], refs[-len(parts) :]
    for out, (away, first, n, at, pass_at) in zip(outs, parts):
        refs = [(passed[i], block) for i, block in pass_at]
        for i in range(n):
            total = merged(away, first, slots, own, arrived, refs, at + i)
            out[i] = total.astype(out.dtype)


def hop(name, parts, slots, own, arrived, passed=()):
    return call(
        functools.partial(hop_kernel, parts),
        name,
        out_shape=[VMEM((p[2], *own.shape[1:]), jnp.bfloat16) for p in parts],
        in_specs=[SMEM_SPEC] + [VMEM_SPEC] * (2 + len(passed)),
        out_specs=[VMEM_SPEC] * len(parts),
    )(keep_scalars(slots), keep(own), arrived, *passed)


def last_kernel(first, slots, own, arrived, passed_a, passed_b, weight, bias, out):
    passed = [(passed_a, 0), (passed_b, 0)]
    for i in range(TPD):
        total = merged(0, first, slots, own, arrived, passed, i).astype(jnp.bfloat16)
        hidden = jnp.dot(total, weight[...], preferred_element_type=jnp.float32) + bias[...]
        out[pl.ds(i * TILE, TILE), :] = jnp.maximum(hidden, 0.0).astype(out.dtype)


def last(slots, own, arrived, passed, weight, bias):
    part, first = arrived
    return call(
        functools.partial(last_kernel, first),
        "last",
        out_shape=jax.ShapeDtypeStruct((ROWS, weight.shape[1]), jnp.bfloat16),
        in_specs=[SMEM_SPEC] + [VMEM_SPEC] * (4 + len(passed)),
        out_specs=VMEM_SPEC,
    )(keep_scalars(slots), keep(own), part, *passed, weight, bias)


def send(array, perm):
    return lax.ppermute(array, "row", perm)


def on_device(node_feats, tile_vals, tile_dest, tile_source, tile_count, weight, out_bias):
    row, col = lax.axis_index("row"), lax.axis_index("col")
    where = jnp.stack(
        [row // (NXLO * NCORE), row // NCORE % NXLO, row % NCORE, col // NXHI, col % NXHI]
    ).astype(jnp.int32)
    slot = jnp.arange(SLOTS, dtype=jnp.int32)[None, :]
    dest = jnp.where(slot < tile_count[0, 0], tile_dest[0], -1)
    up, down, side = (send(node_feats, p) for p in (FROM_UP, FROM_DOWN, FROM_SIDE))
    plan = make_plan(where, dest, tile_source[0])
    up, down, side, plan = lax.optimization_barrier((up, down, side, plan))
    far, down_side, up_side = send(up, FROM_UP), send(side, FROM_DOWN), send(up, FROM_SIDE)
    tiles = load_tiles(tile_vals[0, 0])
    feats = pack(None, 0, [node_feats, up, down, side])
    feats, other, own = first_products(plan, tiles, feats)
    far, down_side, up_side, feats, other, own = lax.optimization_barrier(
        (far, down_side, up_side, feats, other, own)
    )
    partner_dest = lax.ppermute(dest, "col", X_FLIP)
    thirds, at = [], 0
    for n, array, perm in zip(
        THIRDS, (up_side, down_side, far), (FROM_UP, FROM_DOWN, FROM_SIDE)
    ):
        thirds.append(send(array[at : at + n], perm))
        at += n
    feats = pack(feats, EARLY * ROWS, [far, down_side, up_side])
    sibling = send(feats, FROM_CORE)
    kinds = (((1, 0),), ((CLASSES + 1, 0),))
    other, own = more_products("late_products", kinds, plan, tiles, [feats], [other, own])
    thirds, other, own, partner_dest = lax.optimization_barrier((thirds, other, own, partner_dest))
    slots = make_map(where, partner_dest)
    last_feats = join(thirds)
    far_sibling = send(last_feats, FROM_CORE)
    kinds = (((2, 0), (3, 1)),)
    (other,) = more_products("other_half", kinds, plan, tiles, [sibling, last_feats], [other])
    sends = make_sends(plan, tiles, far_sibling, other)
    arrived = {}
    for aways, part in zip(X_PARTS, sends):
        part = lax.ppermute(part, "col", X_FLIP)
        for i, away in enumerate(aways):
            arrived[away] = (part, i * HALF_SLOTS)
    kinds = (tuple((CLASSES + 2 + i, i) for i in range(3)),)
    rest = [sibling, last_feats, far_sibling]
    (own,) = more_products("own_half", kinds, plan, tiles, rest, [own])
    cut = TPD // 2
    parts = ((4, 0, cut, 0, ()), (4, 0, cut, cut, ()))
    chains = hop("hop_4", parts, slots, own, arrived[4][0])
    for a, b in ((3, 5), (2, 6), (1, 7)):
        chains = [lax.ppermute(c, "col", p) for c, p in zip(chains, Z_CHAINS)]
        at = (0, cut if a == 3 else 0)
        chains = [
            hop(
                f"hop_{away}",
                ((away, arrived[away][1], TPD, 0, ((0, at[i]),)),),
                slots,
                own,
                arrived[away][0],
                (c,),
            )[0]
            for i, (away, c) in enumerate(zip((a, b), chains))
        ]
    chains = [lax.ppermute(c, "col", p) for c, p in zip(chains, Z_CHAINS)]
    return last(slots, own, arrived[0], chains, weight, out_bias.reshape(1, -1))


def solution(mesh):
    return jax.shard_map(
        on_device,
        mesh=mesh,
        in_specs=(
            P(("row", "col"), None),
            P("row", "col", None, None, None),
            P("row", "col", None),
            P("row", "col", None),
            P("row", "col"),
            P(),
            P(),
        ),
        out_specs=P(("row", "col"), None),
        check_vma=False,
    )
```

```python
import functools

import jax
import jax.numpy as jnp
from jax import lax
from jax.experimental import pallas as pl
from jax.experimental.pallas import tpu as pltpu
from jax.sharding import PartitionSpec as P

TILE = 128
TPD = 16
SLOTS = 256
NY, NXLO, NCORE = 4, 2, 2
NZ, NXHI = 8, 2
ROWS = TPD * TILE
HALF_SLOTS = 8
OWN_BLOCKS = NZ * TPD
OTHER_BLOCKS = NZ * HALF_SLOTS
GROUP = 16
WIDTH = 512
CLASSES = 5
KINDS = 16
PACKED = ((0, 0), (1, 0), (3, 0), (0, 1), (2, 0), (3, 1), (1, 1), (2, 1))
EARLY = 4
LAST = 7
X_PARTS = ((4,), (3, 5), (2, 6), (1, 7), (0,))
THIRDS = (752, 880, 416)

VMEM = pltpu.VMEM
SMEM_SPEC = pl.BlockSpec(memory_space=pltpu.SMEM)
VMEM_SPEC = pl.BlockSpec(memory_space=pltpu.VMEM)
ANY_SPEC = pl.BlockSpec(memory_space=pl.ANY)


def row_perm(change):
    pairs = []
    for y in range(NY):
        for x in range(NXLO):
            for k in range(NCORE):
                ty, tx, tk = change(y, x, k)
                pairs.append(((y * NXLO + x) * NCORE + k, (ty % NY * NXLO + tx) * NCORE + tk))
    return pairs


FROM_UP = row_perm(lambda y, x, k: (y - 1, x, k))
FROM_DOWN = row_perm(lambda y, x, k: (y + 1, x, k))
FROM_SIDE = row_perm(lambda y, x, k: (y, 1 - x, k))
FROM_CORE = row_perm(lambda y, x, k: (y, x, 1 - k))
Z_PLUS = [(z * NXHI + x, (z + 1) % NZ * NXHI + x) for z in range(NZ) for x in range(NXHI)]
Z_MINUS = [(z * NXHI + x, (z - 1) % NZ * NXHI + x) for z in range(NZ) for x in range(NXHI)]
Z_CHAINS = (Z_PLUS, Z_MINUS)
X_FLIP = [(z * NXHI + x, z * NXHI + 1 - x) for z in range(NZ) for x in range(NXHI)]


def call(kernel, name, **kwargs):
    return pl.pallas_call(
        kernel,
        name=name,
        cost_estimate=pl.CostEstimate(flops=0, bytes_accessed=0, transcendentals=0),
        compiler_params=pltpu.CompilerParams(vmem_limit_bytes=16 << 20),
        **kwargs,
    )


def keep_scalars(array):
    return pltpu.with_memory_space_constraint(array, pltpu.SMEM)


def keep(array):
    return pltpu.with_memory_space_constraint(array, pltpu.VMEM)


def iota(shape, dim):
    return lax.broadcasted_iota(jnp.int32, shape, dim)


def to_column(row):
    n = row.shape[1]
    square = jnp.broadcast_to(row, (n, n))
    return jnp.sum(jnp.where(iota((n, n), 0) == iota((n, n), 1), square, 0.0), 1, keepdims=True)


def to_row(column):
    n = column.shape[0]
    square = jnp.broadcast_to(column, (n, n))
    return jnp.sum(jnp.where(iota((n, n), 0) == iota((n, n), 1), square, 0.0), 0, keepdims=True)


def split_dest(block, my_z):
    block = jnp.maximum(block, 0)
    away = ((block // (NXHI * TPD)) - my_z) & (NZ - 1)
    return away, (block // TPD) & (NXHI - 1), block & (TPD - 1)


def slots_of(key, chosen):
    hit = (iota((OWN_BLOCKS, SLOTS), 0) == key) & chosen
    touched = jnp.max(jnp.where(hit, 1.0, 0.0), axis=1, keepdims=True)
    a, b = iota((OWN_BLOCKS, OWN_BLOCKS), 0), iota((OWN_BLOCKS, OWN_BLOCKS), 1)
    before = (b < a) & (b // TPD == a // TPD)
    rank = jnp.sum(jnp.where(before, to_row(touched), 0.0), axis=1, keepdims=True)
    return hit, touched, rank


def lists_of(kind, value):
    kinds = iota((KINDS, SLOTS), 0)
    n = jnp.sum(jnp.where(kinds == kind, 1, 0).astype(jnp.float32), axis=1, keepdims=True)
    groups = jnp.floor((n + (GROUP - 1)) * (1.0 / GROUP))
    first = jnp.sum(jnp.where(kinds < kind, groups, 0.0), axis=0, keepdims=True) * GROUP
    kind_column = to_column(kind.astype(jnp.float32))
    earlier = iota((SLOTS, SLOTS), 0) < iota((SLOTS, SLOTS), 1)
    same = (kind_column == kind.astype(jnp.float32)) & earlier
    at = first + jnp.sum(jnp.where(same, 1.0, 0.0), axis=0, keepdims=True)
    at = to_column(jnp.where(kind < KINDS, at, -1.0))
    held = at == iota((SLOTS, WIDTH), 1).astype(jnp.float32)
    filled = jnp.sum(jnp.where(held, 1.0, 0.0), axis=0, keepdims=True)
    value = to_column(value.astype(jnp.float32))
    row = jnp.sum(jnp.where(held, value, 0.0), axis=0, keepdims=True).astype(jnp.int32)
    a, b = iota((KINDS, TILE), 0), iota((KINDS, TILE), 1)
    starts = jnp.sum(jnp.where(a < b, groups, 0.0), axis=0, keepdims=True)
    counts = jnp.sum(jnp.where(a == b, groups, 0.0), axis=0, keepdims=True)
    others = jnp.sum(jnp.where(iota((KINDS, 1), 0) < CLASSES, groups, 0.0)) * GROUP
    is_other = iota((1, WIDTH), 1).astype(jnp.float32) < others
    spare = jnp.where(is_other, OTHER_BLOCKS, OWN_BLOCKS) * 65536
    return jnp.where(filled > 0, row, spare), starts.astype(jnp.int32), counts.astype(jnp.int32)


def plan_kernel(where, dest, source, plan):
    my_y, my_x, my_k, my_z, my_xhi = (where[i] for i in range(5))
    block, from_block = dest[...], source[...]
    row = from_block // TPD
    rel = (((row // (NXLO * NCORE)) - my_y) & (NY - 1)) * NXLO
    rel = rel + (((row // NCORE) - my_x) & (NXLO - 1))
    sibling = (row - my_k) & (NCORE - 1)
    slot = jnp.zeros_like(rel)
    for i, (y, x) in enumerate(PACKED):
        slot = jnp.where(rel == y * NXLO + x, i, slot)
    is_far = slot == LAST
    feat = jnp.where(is_far, 0, slot) * TPD + (from_block & (TPD - 1))
    late = jnp.where(slot < EARLY, 0, 1)
    group = jnp.where(is_far, 3 + sibling, jnp.where(sibling == 1, 2, late))
    away, half, inner = split_dest(block, my_z)
    key = away * TPD + inner
    is_own = half == my_xhi
    live = block >= 0
    hit, _, rank = slots_of(key, live & (half != my_xhi))
    slot = jnp.sum(jnp.where(hit, rank, 0.0), axis=0, keepdims=True).astype(jnp.int32)
    to = jnp.where(is_own, key, away * HALF_SLOTS + slot)
    kind = jnp.where(live, jnp.where(is_own, CLASSES, 0) + group, KINDS)
    value = iota((1, SLOTS), 1) + feat * 256 + to * 65536
    row, starts, counts = lists_of(kind, value)
    plan[0:1, :] = row
    plan[1:2, 0:TILE] = starts
    plan[2:3, 0:TILE] = counts


def make_plan(where, dest, source):
    return call(
        plan_kernel,
        "plan",
        out_shape=jax.ShapeDtypeStruct((8, WIDTH), jnp.int32),
        in_specs=[SMEM_SPEC] + [VMEM_SPEC] * 2,
        out_specs=VMEM_SPEC,
    )(where, dest, source)


def map_kernel(where, partner_dest, slots, found, sem):
    my_z, my_xhi = where[3], where[4]
    block = partner_dest[...]
    away, half, inner = split_dest(block, my_z)
    _, touched, rank = slots_of(away * TPD + inner, (block >= 0) & (half == my_xhi))
    slot = to_row(jnp.where(touched > 0, rank, float(HALF_SLOTS)))
    found[...] = slot.astype(jnp.int32)
    copy = pltpu.make_async_copy(found, slots, sem)
    copy.start()
    copy.wait()


def make_map(where, partner_dest):
    return call(
        map_kernel,
        "partner_map",
        out_shape=pltpu.SMEM((1, OWN_BLOCKS), jnp.int32),
        in_specs=[SMEM_SPEC, VMEM_SPEC],
        out_specs=SMEM_SPEC,
        scratch_shapes=[VMEM((1, OWN_BLOCKS), jnp.int32), pltpu.SemaphoreType.DMA(())],
    )(where, partner_dest)


def add_products(plan, kind, tiles, feats, acc):
    def one_group(g, _):
        entries = [plan[0, g * GROUP + i] for i in range(GROUP)]
        products = [
            jnp.dot(
                tiles[e & 255],
                feats[pl.ds(pl.multiple_of(((e >> 8) & 255) * TILE, TILE), TILE), :],
                preferred_element_type=jnp.float32,
            )
            for e in entries
        ]
        for e, product in zip(entries, products):
            acc[e >> 16] += product
        return 0

    first = plan[1, kind]
    lax.fori_loop(first, first + plan[2, kind], one_group, 0)


def clear_blocks(acc, n):
    def clear(i, _):
        acc[i] = jnp.zeros(acc.shape[1:], acc.dtype)
        return 0

    lax.fori_loop(0, n, clear, 0, unroll=4)


def load_tiles_kernel(tiles_hbm, tiles, sem):
    copy = pltpu.make_async_copy(tiles_hbm, tiles, sem)
    copy.start()
    copy.wait()


def load_tiles(tile_set):
    return call(
        load_tiles_kernel,
        "load_tiles",
        out_shape=VMEM(tile_set.shape, tile_set.dtype),
        in_specs=[ANY_SPEC],
        out_specs=VMEM_SPEC,
        scratch_shapes=[pltpu.SemaphoreType.DMA(())],
    )(tile_set)


def pack_kernel(has_base, first, *refs):
    packed = refs[-1]
    for i, ref in enumerate(refs[has_base:-1]):
        packed[pl.ds(first + i * ROWS, ROWS), :] = ref[...]


def pack(base, first, arrays):
    has_base = base is not None
    return call(
        functools.partial(pack_kernel, has_base, first),
        "pack",
        out_shape=VMEM((LAST * ROWS, arrays[0].shape[1]), arrays[0].dtype),
        in_specs=[VMEM_SPEC] * (has_base + len(arrays)),
        out_specs=VMEM_SPEC,
        input_output_aliases={0: 0} if has_base else {},
    )(*([keep(base)] if has_base else []), *arrays)


def join_kernel(*refs):
    at = 0
    for ref in refs[:-1]:
        refs[-1][pl.ds(at, ref.shape[0]), :] = ref[...]
        at += ref.shape[0]


def join(arrays):
    return call(
        join_kernel,
        "join",
        out_shape=VMEM((ROWS, arrays[0].shape[1]), arrays[0].dtype),
        in_specs=[VMEM_SPEC] * len(arrays),
        out_specs=VMEM_SPEC,
    )(*arrays)


def first_kernel(plan, tiles, feats, _, other, own):
    clear_blocks(other, OTHER_BLOCKS)
    clear_blocks(own, OWN_BLOCKS)
    add_products(plan, 0, tiles, feats, other)
    add_products(plan, CLASSES, tiles, feats, own)


def first_products(plan, tiles, feats):
    block = (TILE, feats.shape[1])
    return call(
        first_kernel,
        "first_products",
        out_shape=[
            VMEM(feats.shape, feats.dtype),
            VMEM((OTHER_BLOCKS + 1, *block), jnp.float32),
            VMEM((OWN_BLOCKS + 1, *block), jnp.float32),
        ],
        in_specs=[SMEM_SPEC] + [VMEM_SPEC] * 2,
        out_specs=[VMEM_SPEC] * 3,
        input_output_aliases={2: 0},
    )(plan, keep(tiles), keep(feats))


def more_kernel(kinds, n_feats, plan, tiles, *refs):
    feats, accs = refs[:n_feats], refs[-len(kinds) :]
    for acc, of_acc in zip(accs, kinds):
        for kind, at in of_acc:
            add_products(plan, kind, tiles, feats[at], acc)


def more_products(name, kinds, plan, tiles, feats, accs):
    n = 2 + len(feats)
    return call(
        functools.partial(more_kernel, kinds, len(feats)),
        name,
        out_shape=[VMEM(acc.shape, acc.dtype) for acc in accs],
        in_specs=[SMEM_SPEC] + [VMEM_SPEC] * (n - 1 + len(accs)),
        out_specs=[VMEM_SPEC] * len(accs),
        input_output_aliases={n + i: i for i in range(len(accs))},
    )(plan, keep(tiles), *[keep(f) for f in feats], *[keep(acc) for acc in accs])


def convert_sends(acc, parts, sends):
    for aways, send in zip(parts, sends):
        for i, away in enumerate(aways):
            blocks = acc[pl.ds(away * HALF_SLOTS, HALF_SLOTS)]
            send[pl.ds(i * HALF_SLOTS, HALF_SLOTS)] = blocks.astype(send.dtype)


def first_send_kernel(plan, tiles, far_sibling, _, acc, send):
    add_products(plan, 4, tiles, far_sibling, acc)
    convert_sends(acc, X_PARTS[:1], [send])


def sends_kernel(acc, *sends):
    convert_sends(acc, X_PARTS[1:], sends)


def make_sends(plan, tiles, far_sibling, acc):
    part = lambda p: VMEM((HALF_SLOTS * len(p), *acc.shape[1:]), jnp.bfloat16)
    acc, first = call(
        first_send_kernel,
        "first_send",
        out_shape=[VMEM(acc.shape, acc.dtype), part(X_PARTS[0])],
        in_specs=[SMEM_SPEC] + [VMEM_SPEC] * 3,
        out_specs=[VMEM_SPEC] * 2,
        input_output_aliases={3: 0},
    )(plan, keep(tiles), keep(far_sibling), keep(acc))
    rest = call(
        sends_kernel,
        "other_sends",
        out_shape=[part(p) for p in X_PARTS[1:]],
        in_specs=[VMEM_SPEC],
        out_specs=[VMEM_SPEC] * (len(X_PARTS) - 1),
    )(keep(acc))
    return [first, *rest]


def merged(away, first, slots, own, arrived, passed, i):
    total = own[away * TPD + i]
    for ref, at in passed:
        if at <= i < at + ref.shape[0]:
            total += ref[i - at].astype(jnp.float32)
    slot = slots[0, away * TPD + i]
    seen = (slot < HALF_SLOTS).astype(jnp.float32)
    block = arrived[first + jnp.minimum(slot, HALF_SLOTS - 1)]
    return total + block.astype(jnp.float32) * seen


def hop_kernel(parts, slots, own, arrived, *refs):
    passed, outs = refs[: -len(parts)], refs[-len(parts) :]
    for out, (away, first, n, at, pass_at) in zip(outs, parts):
        refs = [(passed[i], block) for i, block in pass_at]
        for i in range(n):
            total = merged(away, first, slots, own, arrived, refs, at + i)
            out[i] = total.astype(out.dtype)


def hop(name, parts, slots, own, arrived, passed=()):
    return call(
        functools.partial(hop_kernel, parts),
        name,
        out_shape=[VMEM((p[2], *own.shape[1:]), jnp.bfloat16) for p in parts],
        in_specs=[SMEM_SPEC] + [VMEM_SPEC] * (2 + len(passed)),
        out_specs=[VMEM_SPEC] * len(parts),
    )(keep_scalars(slots), keep(own), arrived, *passed)


def last_kernel(first, slots, own, arrived, passed_a, passed_b, weight, bias, out):
    passed = [(passed_a, 0), (passed_b, 0)]
    for i in range(TPD):
        total = merged(0, first, slots, own, arrived, passed, i).astype(jnp.bfloat16)
        hidden = jnp.dot(total, weight[...], preferred_element_type=jnp.float32) + bias[...]
        out[pl.ds(i * TILE, TILE), :] = jnp.maximum(hidden, 0.0).astype(out.dtype)


def last(slots, own, arrived, passed, weight, bias):
    part, first = arrived
    return call(
        functools.partial(last_kernel, first),
        "last",
        out_shape=jax.ShapeDtypeStruct((ROWS, weight.shape[1]), jnp.bfloat16),
        in_specs=[SMEM_SPEC] + [VMEM_SPEC] * (4 + len(passed)),
        out_specs=VMEM_SPEC,
    )(keep_scalars(slots), keep(own), part, *passed, weight, bias)


def send(array, perm):
    return lax.ppermute(array, "row", perm)


def on_device(node_feats, tile_vals, tile_dest, tile_source, tile_count, weight, out_bias):
    row, col = lax.axis_index("row"), lax.axis_index("col")
    where = jnp.stack(
        [row // (NXLO * NCORE), row // NCORE % NXLO, row % NCORE, col // NXHI, col % NXHI]
    ).astype(jnp.int32)
    slot = jnp.arange(SLOTS, dtype=jnp.int32)[None, :]
    dest = jnp.where(slot < tile_count[0, 0], tile_dest[0], -1)
    up, down, side = (send(node_feats, p) for p in (FROM_UP, FROM_DOWN, FROM_SIDE))
    plan = make_plan(where, dest, tile_source[0])
    up, down, side, plan = lax.optimization_barrier((up, down, side, plan))
    far, down_side, up_side = send(up, FROM_UP), send(side, FROM_DOWN), send(up, FROM_SIDE)
    tiles = load_tiles(tile_vals[0, 0])
    feats = pack(None, 0, [node_feats, up, down, side])
    feats, other, own = first_products(plan, tiles, feats)
    far, down_side, up_side, feats, other, own = lax.optimization_barrier(
        (far, down_side, up_side, feats, other, own)
    )
    partner_dest = lax.ppermute(dest, "col", X_FLIP)
    thirds, at = [], 0
    for n, array, perm in zip(
        THIRDS, (up_side, down_side, far), (FROM_UP, FROM_DOWN, FROM_SIDE)
    ):
        thirds.append(send(array[at : at + n], perm))
        at += n
    feats = pack(feats, EARLY * ROWS, [far, down_side, up_side])
    sibling = send(feats, FROM_CORE)
    kinds = (((1, 0),), ((CLASSES + 1, 0),))
    other, own = more_products("late_products", kinds, plan, tiles, [feats], [other, own])
    thirds, other, own, partner_dest = lax.optimization_barrier((thirds, other, own, partner_dest))
    slots = make_map(where, partner_dest)
    last_feats = join(thirds)
    far_sibling = send(last_feats, FROM_CORE)
    kinds = (((2, 0), (3, 1)),)
    (other,) = more_products("other_half", kinds, plan, tiles, [sibling, last_feats], [other])
    sends = make_sends(plan, tiles, far_sibling, other)
    arrived = {}
    for aways, part in zip(X_PARTS, sends):
        part = lax.ppermute(part, "col", X_FLIP)
        for i, away in enumerate(aways):
            arrived[away] = (part, i * HALF_SLOTS)
    kinds = (tuple((CLASSES + 2 + i, i) for i in range(3)),)
    rest = [sibling, last_feats, far_sibling]
    (own,) = more_products("own_half", kinds, plan, tiles, rest, [own])
    cut = TPD // 2
    parts = ((4, 0, cut, 0, ()), (4, 0, cut, cut, ()))
    chains = hop("hop_4", parts, slots, own, arrived[4][0])
    for a, b in ((3, 5), (2, 6), (1, 7)):
        chains = [lax.ppermute(c, "col", p) for c, p in zip(chains, Z_CHAINS)]
        at = (0, cut if a == 3 else 0)
        chains = [
            hop(
                f"hop_{away}",
                ((away, arrived[away][1], TPD, 0, ((0, at[i]),)),),
                slots,
                own,
                arrived[away][0],
                (c,),
            )[0]
            for i, (away, c) in enumerate(zip((a, b), chains))
        ]
    chains = [lax.ppermute(c, "col", p) for c, p in zip(chains, Z_CHAINS)]
    return last(slots, own, arrived[0], chains, weight, out_bias.reshape(1, -1))


def solution(mesh):
    return jax.shard_map(
        on_device,
        mesh=mesh,
        in_specs=(
            P(("row", "col"), None),
            P("row", "col", None, None, None),
            P("row", "col", None),
            P("row", "col", None),
            P("row", "col"),
            P(),
            P(),
        ),
        out_specs=P(("row", "col"), None),
        check_vma=False,
    )
```

```python
import functools

import jax
import jax.numpy as jnp
from jax import lax
from jax.experimental import pallas as pl
from jax.experimental.pallas import tpu as pltpu
from jax.sharding import PartitionSpec as P

TILE = 128
TPD = 16
SLOTS = 256
NY, NXLO, NCORE = 4, 2, 2
NZ, NXHI = 8, 2
ROWS = TPD * TILE
HALF_SLOTS = 8
OWN_BLOCKS = NZ * TPD
OTHER_BLOCKS = NZ * HALF_SLOTS
GROUP = 16
WIDTH = 512
CLASSES = 5
KINDS = 16
PACKED = ((0, 0), (1, 0), (3, 0), (0, 1), (2, 0), (3, 1), (1, 1), (2, 1))
EARLY = 4
LAST = 7
X_PARTS = ((4,), (3,), (5,), (2, 6), (1, 7), (0,))
THIRDS = (752, 880, 416)

VMEM = pltpu.VMEM
SMEM_SPEC = pl.BlockSpec(memory_space=pltpu.SMEM)
VMEM_SPEC = pl.BlockSpec(memory_space=pltpu.VMEM)
ANY_SPEC = pl.BlockSpec(memory_space=pl.ANY)


def row_perm(change):
    pairs = []
    for y in range(NY):
        for x in range(NXLO):
            for k in range(NCORE):
                ty, tx, tk = change(y, x, k)
                pairs.append(((y * NXLO + x) * NCORE + k, (ty % NY * NXLO + tx) * NCORE + tk))
    return pairs


FROM_UP = row_perm(lambda y, x, k: (y - 1, x, k))
FROM_DOWN = row_perm(lambda y, x, k: (y + 1, x, k))
FROM_SIDE = row_perm(lambda y, x, k: (y, 1 - x, k))
FROM_CORE = row_perm(lambda y, x, k: (y, x, 1 - k))
Z_PLUS = [(z * NXHI + x, (z + 1) % NZ * NXHI + x) for z in range(NZ) for x in range(NXHI)]
Z_MINUS = [(z * NXHI + x, (z - 1) % NZ * NXHI + x) for z in range(NZ) for x in range(NXHI)]
Z_CHAINS = (Z_PLUS, Z_MINUS)
X_FLIP = [(z * NXHI + x, z * NXHI + 1 - x) for z in range(NZ) for x in range(NXHI)]


def call(kernel, name, **kwargs):
    return pl.pallas_call(
        kernel,
        name=name,
        cost_estimate=pl.CostEstimate(flops=0, bytes_accessed=0, transcendentals=0),
        compiler_params=pltpu.CompilerParams(vmem_limit_bytes=16 << 20),
        **kwargs,
    )


def keep_scalars(array):
    return pltpu.with_memory_space_constraint(array, pltpu.SMEM)


def keep(array):
    return pltpu.with_memory_space_constraint(array, pltpu.VMEM)


def iota(shape, dim):
    return lax.broadcasted_iota(jnp.int32, shape, dim)


def to_column(row):
    n = row.shape[1]
    square = jnp.broadcast_to(row, (n, n))
    return jnp.sum(jnp.where(iota((n, n), 0) == iota((n, n), 1), square, 0.0), 1, keepdims=True)


def to_row(column):
    n = column.shape[0]
    square = jnp.broadcast_to(column, (n, n))
    return jnp.sum(jnp.where(iota((n, n), 0) == iota((n, n), 1), square, 0.0), 0, keepdims=True)


def split_dest(block, my_z):
    block = jnp.maximum(block, 0)
    away = ((block // (NXHI * TPD)) - my_z) & (NZ - 1)
    return away, (block // TPD) & (NXHI - 1), block & (TPD - 1)


def slots_of(key, chosen):
    hit = (iota((OWN_BLOCKS, SLOTS), 0) == key) & chosen
    touched = jnp.max(jnp.where(hit, 1.0, 0.0), axis=1, keepdims=True)
    a, b = iota((OWN_BLOCKS, OWN_BLOCKS), 0), iota((OWN_BLOCKS, OWN_BLOCKS), 1)
    before = (b < a) & (b // TPD == a // TPD)
    rank = jnp.sum(jnp.where(before, to_row(touched), 0.0), axis=1, keepdims=True)
    return hit, touched, rank


def lists_of(kind, value):
    kinds = iota((KINDS, SLOTS), 0)
    n = jnp.sum(jnp.where(kinds == kind, 1, 0).astype(jnp.float32), axis=1, keepdims=True)
    groups = jnp.floor((n + (GROUP - 1)) * (1.0 / GROUP))
    first = jnp.sum(jnp.where(kinds < kind, groups, 0.0), axis=0, keepdims=True) * GROUP
    kind_column = to_column(kind.astype(jnp.float32))
    earlier = iota((SLOTS, SLOTS), 0) < iota((SLOTS, SLOTS), 1)
    same = (kind_column == kind.astype(jnp.float32)) & earlier
    at = first + jnp.sum(jnp.where(same, 1.0, 0.0), axis=0, keepdims=True)
    at = to_column(jnp.where(kind < KINDS, at, -1.0))
    held = at == iota((SLOTS, WIDTH), 1).astype(jnp.float32)
    filled = jnp.sum(jnp.where(held, 1.0, 0.0), axis=0, keepdims=True)
    value = to_column(value.astype(jnp.float32))
    row = jnp.sum(jnp.where(held, value, 0.0), axis=0, keepdims=True).astype(jnp.int32)
    a, b = iota((KINDS, TILE), 0), iota((KINDS, TILE), 1)
    starts = jnp.sum(jnp.where(a < b, groups, 0.0), axis=0, keepdims=True)
    counts = jnp.sum(jnp.where(a == b, groups, 0.0), axis=0, keepdims=True)
    others = jnp.sum(jnp.where(iota((KINDS, 1), 0) < CLASSES, groups, 0.0)) * GROUP
    is_other = iota((1, WIDTH), 1).astype(jnp.float32) < others
    spare = jnp.where(is_other, OTHER_BLOCKS, OWN_BLOCKS) * 65536
    return jnp.where(filled > 0, row, spare), starts.astype(jnp.int32), counts.astype(jnp.int32)


def plan_kernel(where, dest, source, plan):
    my_y, my_x, my_k, my_z, my_xhi = (where[i] for i in range(5))
    block, from_block = dest[...], source[...]
    row = from_block // TPD
    rel = (((row // (NXLO * NCORE)) - my_y) & (NY - 1)) * NXLO
    rel = rel + (((row // NCORE) - my_x) & (NXLO - 1))
    sibling = (row - my_k) & (NCORE - 1)
    slot = jnp.zeros_like(rel)
    for i, (y, x) in enumerate(PACKED):
        slot = jnp.where(rel == y * NXLO + x, i, slot)
    is_far = slot == LAST
    feat = jnp.where(is_far, 0, slot) * TPD + (from_block & (TPD - 1))
    late = jnp.where(slot < EARLY, 0, 1)
    group = jnp.where(is_far, 3 + sibling, jnp.where(sibling == 1, 2, late))
    away, half, inner = split_dest(block, my_z)
    key = away * TPD + inner
    is_own = half == my_xhi
    live = block >= 0
    hit, _, rank = slots_of(key, live & (half != my_xhi))
    slot = jnp.sum(jnp.where(hit, rank, 0.0), axis=0, keepdims=True).astype(jnp.int32)
    to = jnp.where(is_own, key, away * HALF_SLOTS + slot)
    kind = jnp.where(live, jnp.where(is_own, CLASSES, 0) + group, KINDS)
    value = iota((1, SLOTS), 1) + feat * 256 + to * 65536
    row, starts, counts = lists_of(kind, value)
    plan[0:1, :] = row
    plan[1:2, 0:TILE] = starts
    plan[2:3, 0:TILE] = counts


def make_plan(where, dest, source):
    return call(
        plan_kernel,
        "plan",
        out_shape=jax.ShapeDtypeStruct((8, WIDTH), jnp.int32),
        in_specs=[SMEM_SPEC] + [VMEM_SPEC] * 2,
        out_specs=VMEM_SPEC,
    )(where, dest, source)


def map_kernel(where, partner_dest, slots, found, sem):
    my_z, my_xhi = where[3], where[4]
    block = partner_dest[...]
    away, half, inner = split_dest(block, my_z)
    _, touched, rank = slots_of(away * TPD + inner, (block >= 0) & (half == my_xhi))
    slot = to_row(jnp.where(touched > 0, rank, float(HALF_SLOTS)))
    found[...] = slot.astype(jnp.int32)
    copy = pltpu.make_async_copy(found, slots, sem)
    copy.start()
    copy.wait()


def make_map(where, partner_dest):
    return call(
        map_kernel,
        "partner_map",
        out_shape=pltpu.SMEM((1, OWN_BLOCKS), jnp.int32),
        in_specs=[SMEM_SPEC, VMEM_SPEC],
        out_specs=SMEM_SPEC,
        scratch_shapes=[VMEM((1, OWN_BLOCKS), jnp.int32), pltpu.SemaphoreType.DMA(())],
    )(where, partner_dest)


def add_products(plan, kind, tiles, feats, acc):
    def one_group(g, _):
        entries = [plan[0, g * GROUP + i] for i in range(GROUP)]
        products = [
            jnp.dot(
                tiles[e & 255],
                feats[pl.ds(pl.multiple_of(((e >> 8) & 255) * TILE, TILE), TILE), :],
                preferred_element_type=jnp.float32,
            )
            for e in entries
        ]
        for e, product in zip(entries, products):
            acc[e >> 16] += product
        return 0

    first = plan[1, kind]
    lax.fori_loop(first, first + plan[2, kind], one_group, 0)


def clear_blocks(acc, n):
    def clear(i, _):
        acc[i] = jnp.zeros(acc.shape[1:], acc.dtype)
        return 0

    lax.fori_loop(0, n, clear, 0, unroll=4)


def load_tiles_kernel(tiles_hbm, tiles, sem):
    copy = pltpu.make_async_copy(tiles_hbm, tiles, sem)
    copy.start()
    copy.wait()


def load_tiles(tile_set):
    return call(
        load_tiles_kernel,
        "load_tiles",
        out_shape=VMEM(tile_set.shape, tile_set.dtype),
        in_specs=[ANY_SPEC],
        out_specs=VMEM_SPEC,
        scratch_shapes=[pltpu.SemaphoreType.DMA(())],
    )(tile_set)


def pack_kernel(has_base, first, *refs):
    packed = refs[-1]
    for i, ref in enumerate(refs[has_base:-1]):
        packed[pl.ds(first + i * ROWS, ROWS), :] = ref[...]


def pack(base, first, arrays):
    has_base = base is not None
    return call(
        functools.partial(pack_kernel, has_base, first),
        "pack",
        out_shape=VMEM((LAST * ROWS, arrays[0].shape[1]), arrays[0].dtype),
        in_specs=[VMEM_SPEC] * (has_base + len(arrays)),
        out_specs=VMEM_SPEC,
        input_output_aliases={0: 0} if has_base else {},
    )(*([keep(base)] if has_base else []), *arrays)


def pack_second_kernel(_, up_side, down_side, far, packed, *thirds):
    for i, ref in enumerate((far, down_side, up_side)):
        packed[pl.ds((EARLY + i) * ROWS, ROWS), :] = ref[...]
    at = 0
    for n, ref, third in zip(THIRDS, (up_side, down_side, far), thirds):
        third[...] = ref[pl.ds(at, n), :]
        at += n


def pack_second(base, arrays):
    width = base.shape[1]
    packed, *thirds = call(
        pack_second_kernel,
        "pack_second",
        out_shape=[VMEM(base.shape, base.dtype)] + [VMEM((n, width), base.dtype) for n in THIRDS],
        in_specs=[VMEM_SPEC] * 4,
        out_specs=[VMEM_SPEC] * 4,
        input_output_aliases={0: 0},
    )(keep(base), *arrays)
    return packed, thirds


def join_kernel(*refs):
    at = 0
    for ref in refs[:-1]:
        refs[-1][pl.ds(at, ref.shape[0]), :] = ref[...]
        at += ref.shape[0]


def join(arrays):
    return call(
        join_kernel,
        "join",
        out_shape=VMEM((ROWS, arrays[0].shape[1]), arrays[0].dtype),
        in_specs=[VMEM_SPEC] * len(arrays),
        out_specs=VMEM_SPEC,
    )(*arrays)


def first_kernel(plan, tiles, feats, _, other, own):
    clear_blocks(other, OTHER_BLOCKS)
    clear_blocks(own, OWN_BLOCKS)
    add_products(plan, 0, tiles, feats, other)
    add_products(plan, CLASSES, tiles, feats, own)


def first_products(plan, tiles, feats):
    block = (TILE, feats.shape[1])
    return call(
        first_kernel,
        "first_products",
        out_shape=[
            VMEM(feats.shape, feats.dtype),
            VMEM((OTHER_BLOCKS + 1, *block), jnp.float32),
            VMEM((OWN_BLOCKS + 1, *block), jnp.float32),
        ],
        in_specs=[SMEM_SPEC] + [VMEM_SPEC] * 2,
        out_specs=[VMEM_SPEC] * 3,
        input_output_aliases={2: 0},
    )(plan, keep(tiles), keep(feats))


def more_kernel(kinds, n_feats, plan, tiles, *refs):
    feats, accs = refs[:n_feats], refs[-len(kinds) :]
    for acc, of_acc in zip(accs, kinds):
        for kind, at in of_acc:
            add_products(plan, kind, tiles, feats[at], acc)


def more_products(name, kinds, plan, tiles, feats, accs):
    n = 2 + len(feats)
    return call(
        functools.partial(more_kernel, kinds, len(feats)),
        name,
        out_shape=[VMEM(acc.shape, acc.dtype) for acc in accs],
        in_specs=[SMEM_SPEC] + [VMEM_SPEC] * (n - 1 + len(accs)),
        out_specs=[VMEM_SPEC] * len(accs),
        input_output_aliases={n + i: i for i in range(len(accs))},
    )(plan, keep(tiles), *[keep(f) for f in feats], *[keep(acc) for acc in accs])


def convert_sends(acc, parts, sends):
    for aways, send in zip(parts, sends):
        for i, away in enumerate(aways):
            blocks = acc[pl.ds(away * HALF_SLOTS, HALF_SLOTS)]
            send[pl.ds(i * HALF_SLOTS, HALF_SLOTS)] = blocks.astype(send.dtype)


def first_send_kernel(plan, tiles, far_sibling, _, acc, send):
    add_products(plan, 4, tiles, far_sibling, acc)
    convert_sends(acc, X_PARTS[:1], [send])


def sends_kernel(acc, *sends):
    convert_sends(acc, X_PARTS[1:], sends)


def make_sends(plan, tiles, far_sibling, acc):
    part = lambda p: VMEM((HALF_SLOTS * len(p), *acc.shape[1:]), jnp.bfloat16)
    acc, first = call(
        first_send_kernel,
        "first_send",
        out_shape=[VMEM(acc.shape, acc.dtype), part(X_PARTS[0])],
        in_specs=[SMEM_SPEC] + [VMEM_SPEC] * 3,
        out_specs=[VMEM_SPEC] * 2,
        input_output_aliases={3: 0},
    )(plan, keep(tiles), keep(far_sibling), keep(acc))
    rest = call(
        sends_kernel,
        "other_sends",
        out_shape=[part(p) for p in X_PARTS[1:]],
        in_specs=[VMEM_SPEC],
        out_specs=[VMEM_SPEC] * (len(X_PARTS) - 1),
    )(keep(acc))
    return [first, *rest]


def merged(away, first, slots, own, arrived, passed, i):
    total = own[away * TPD + i]
    for ref, at in passed:
        if at <= i < at + ref.shape[0]:
            total += ref[i - at].astype(jnp.float32)
    slot = slots[0, away * TPD + i]
    seen = (slot < HALF_SLOTS).astype(jnp.float32)
    block = arrived[first + jnp.minimum(slot, HALF_SLOTS - 1)]
    return total + block.astype(jnp.float32) * seen


def hop_kernel(parts, slots, own, arrived, *refs):
    passed, outs = refs[: -len(parts)], refs[-len(parts) :]
    for out, (away, first, n, at, pass_at) in zip(outs, parts):
        refs = [(passed[i], block) for i, block in pass_at]
        for i in range(n):
            total = merged(away, first, slots, own, arrived, refs, at + i)
            out[i] = total.astype(out.dtype)


def hop(name, parts, slots, own, arrived, passed=()):
    return call(
        functools.partial(hop_kernel, parts),
        name,
        out_shape=[VMEM((p[2], *own.shape[1:]), jnp.bfloat16) for p in parts],
        in_specs=[SMEM_SPEC] + [VMEM_SPEC] * (2 + len(passed)),
        out_specs=[VMEM_SPEC] * len(parts),
    )(keep_scalars(slots), keep(own), arrived, *passed)


def last_kernel(first, slots, own, arrived, passed_a, passed_b, weight, bias, out):
    passed = [(passed_a, 0), (passed_b, 0)]
    for i in range(TPD):
        total = merged(0, first, slots, own, arrived, passed, i).astype(jnp.bfloat16)
        hidden = jnp.dot(total, weight[...], preferred_element_type=jnp.float32) + bias[...]
        out[pl.ds(i * TILE, TILE), :] = jnp.maximum(hidden, 0.0).astype(out.dtype)


def last(slots, own, arrived, passed, weight, bias):
    part, first = arrived
    return call(
        functools.partial(last_kernel, first),
        "last",
        out_shape=jax.ShapeDtypeStruct((ROWS, weight.shape[1]), jnp.bfloat16),
        in_specs=[SMEM_SPEC] + [VMEM_SPEC] * (4 + len(passed)),
        out_specs=VMEM_SPEC,
    )(keep_scalars(slots), keep(own), part, *passed, weight, bias)


def send(array, perm):
    return lax.ppermute(array, "row", perm)


def on_device(node_feats, tile_vals, tile_dest, tile_source, tile_count, weight, out_bias):
    row, col = lax.axis_index("row"), lax.axis_index("col")
    where = jnp.stack(
        [row // (NXLO * NCORE), row // NCORE % NXLO, row % NCORE, col // NXHI, col % NXHI]
    ).astype(jnp.int32)
    slot = jnp.arange(SLOTS, dtype=jnp.int32)[None, :]
    dest = jnp.where(slot < tile_count[0, 0], tile_dest[0], -1)
    up, down, side = (send(node_feats, p) for p in (FROM_UP, FROM_DOWN, FROM_SIDE))
    plan = make_plan(where, dest, tile_source[0])
    up, down, side, plan = lax.optimization_barrier((up, down, side, plan))
    far, down_side, up_side = send(up, FROM_UP), send(side, FROM_DOWN), send(up, FROM_SIDE)
    tiles = load_tiles(tile_vals[0, 0])
    feats = pack(None, 0, [node_feats, up, down, side])
    feats, other, own = first_products(plan, tiles, feats)
    far, down_side, up_side, feats, other, own = lax.optimization_barrier(
        (far, down_side, up_side, feats, other, own)
    )
    partner_dest = lax.ppermute(dest, "col", X_FLIP)
    feats, parts = pack_second(feats, (up_side, down_side, far))
    thirds = [send(p, perm) for p, perm in zip(parts, (FROM_UP, FROM_DOWN, FROM_SIDE))]
    sibling = send(feats, FROM_CORE)
    kinds = (((1, 0),), ((CLASSES + 1, 0),))
    other, own = more_products("late_products", kinds, plan, tiles, [feats], [other, own])
    thirds, other, own, partner_dest = lax.optimization_barrier((thirds, other, own, partner_dest))
    slots = make_map(where, partner_dest)
    last_feats = join(thirds)
    far_sibling = send(last_feats, FROM_CORE)
    kinds = (((2, 0), (3, 1)),)
    (other,) = more_products("other_half", kinds, plan, tiles, [sibling, last_feats], [other])
    sends = make_sends(plan, tiles, far_sibling, other)
    arrived = {}
    for aways, part in zip(X_PARTS, sends):
        part = lax.ppermute(part, "col", X_FLIP)
        for i, away in enumerate(aways):
            arrived[away] = (part, i * HALF_SLOTS)
    kinds = (tuple((CLASSES + 2 + i, i) for i in range(3)),)
    rest = [sibling, last_feats, far_sibling]
    (own,) = more_products("own_half", kinds, plan, tiles, rest, [own])
    cut = TPD // 2
    parts = ((4, 0, cut, 0, ()), (4, 0, cut, cut, ()))
    chains = hop("hop_4", parts, slots, own, arrived[4][0])
    for a, b in ((3, 5), (2, 6), (1, 7)):
        chains = [lax.ppermute(c, "col", p) for c, p in zip(chains, Z_CHAINS)]
        at = (0, cut if a == 3 else 0)
        chains = [
            hop(
                f"hop_{away}",
                ((away, arrived[away][1], TPD, 0, ((0, at[i]),)),),
                slots,
                own,
                arrived[away][0],
                (c,),
            )[0]
            for i, (away, c) in enumerate(zip((a, b), chains))
        ]
    chains = [lax.ppermute(c, "col", p) for c, p in zip(chains, Z_CHAINS)]
    return last(slots, own, arrived[0], chains, weight, out_bias.reshape(1, -1))


def solution(mesh):
    return jax.shard_map(
        on_device,
        mesh=mesh,
        in_specs=(
            P(("row", "col"), None),
            P("row", "col", None, None, None),
            P("row", "col", None),
            P("row", "col", None),
            P("row", "col"),
            P(),
            P(),
        ),
        out_specs=P(("row", "col"), None),
        check_vma=False,
    )
```

```python
import functools

import jax
import jax.numpy as jnp
from jax import lax
from jax.experimental import pallas as pl
from jax.experimental.pallas import tpu as pltpu
from jax.sharding import PartitionSpec as P

TILE = 128
TPD = 16
SLOTS = 256
NY, NXLO, NCORE = 4, 2, 2
NZ, NXHI = 8, 2
ROWS = TPD * TILE
HALF_SLOTS = 8
OWN_BLOCKS = NZ * TPD
OTHER_BLOCKS = NZ * HALF_SLOTS
GROUP = 16
WIDTH = 512
CLASSES = 5
KINDS = 16
PACKED = ((0, 0), (1, 0), (3, 0), (0, 1), (2, 0), (3, 1), (1, 1), (2, 1))
EARLY = 4
LAST = 7
X_PARTS = ((4,), (3,), (5,), (2, 6), (1, 7), (0,))
THIRDS = (752, 880, 416)

VMEM = pltpu.VMEM
SMEM_SPEC = pl.BlockSpec(memory_space=pltpu.SMEM)
VMEM_SPEC = pl.BlockSpec(memory_space=pltpu.VMEM)
ANY_SPEC = pl.BlockSpec(memory_space=pl.ANY)


def row_perm(change):
    pairs = []
    for y in range(NY):
        for x in range(NXLO):
            for k in range(NCORE):
                ty, tx, tk = change(y, x, k)
                pairs.append(((y * NXLO + x) * NCORE + k, (ty % NY * NXLO + tx) * NCORE + tk))
    return pairs


FROM_UP = row_perm(lambda y, x, k: (y - 1, x, k))
FROM_DOWN = row_perm(lambda y, x, k: (y + 1, x, k))
FROM_SIDE = row_perm(lambda y, x, k: (y, 1 - x, k))
FROM_CORE = row_perm(lambda y, x, k: (y, x, 1 - k))
Z_PLUS = [(z * NXHI + x, (z + 1) % NZ * NXHI + x) for z in range(NZ) for x in range(NXHI)]
Z_MINUS = [(z * NXHI + x, (z - 1) % NZ * NXHI + x) for z in range(NZ) for x in range(NXHI)]
Z_CHAINS = (Z_PLUS, Z_MINUS)
X_FLIP = [(z * NXHI + x, z * NXHI + 1 - x) for z in range(NZ) for x in range(NXHI)]


def call(kernel, name, **kwargs):
    return pl.pallas_call(
        kernel,
        name=name,
        cost_estimate=pl.CostEstimate(flops=0, bytes_accessed=0, transcendentals=0),
        compiler_params=pltpu.CompilerParams(vmem_limit_bytes=16 << 20),
        **kwargs,
    )


def keep_scalars(array):
    return pltpu.with_memory_space_constraint(array, pltpu.SMEM)


def keep(array):
    return pltpu.with_memory_space_constraint(array, pltpu.VMEM)


def iota(shape, dim):
    return lax.broadcasted_iota(jnp.int32, shape, dim)


def to_column(row):
    n = row.shape[1]
    square = jnp.broadcast_to(row, (n, n))
    return jnp.sum(jnp.where(iota((n, n), 0) == iota((n, n), 1), square, 0.0), 1, keepdims=True)


def to_row(column):
    n = column.shape[0]
    square = jnp.broadcast_to(column, (n, n))
    return jnp.sum(jnp.where(iota((n, n), 0) == iota((n, n), 1), square, 0.0), 0, keepdims=True)


def split_dest(block, my_z):
    block = jnp.maximum(block, 0)
    away = ((block // (NXHI * TPD)) - my_z) & (NZ - 1)
    return away, (block // TPD) & (NXHI - 1), block & (TPD - 1)


def slots_of(key, chosen):
    hit = (iota((OWN_BLOCKS, SLOTS), 0) == key) & chosen
    touched = jnp.max(jnp.where(hit, 1.0, 0.0), axis=1, keepdims=True)
    a, b = iota((OWN_BLOCKS, OWN_BLOCKS), 0), iota((OWN_BLOCKS, OWN_BLOCKS), 1)
    before = (b < a) & (b // TPD == a // TPD)
    rank = jnp.sum(jnp.where(before, to_row(touched), 0.0), axis=1, keepdims=True)
    return hit, touched, rank


def lists_of(kind, value):
    kinds = iota((KINDS, SLOTS), 0)
    n = jnp.sum(jnp.where(kinds == kind, 1, 0).astype(jnp.float32), axis=1, keepdims=True)
    groups = jnp.floor((n + (GROUP - 1)) * (1.0 / GROUP))
    first = jnp.sum(jnp.where(kinds < kind, groups, 0.0), axis=0, keepdims=True) * GROUP
    kind_column = to_column(kind.astype(jnp.float32))
    earlier = iota((SLOTS, SLOTS), 0) < iota((SLOTS, SLOTS), 1)
    same = (kind_column == kind.astype(jnp.float32)) & earlier
    at = first + jnp.sum(jnp.where(same, 1.0, 0.0), axis=0, keepdims=True)
    at = to_column(jnp.where(kind < KINDS, at, -1.0))
    held = at == iota((SLOTS, WIDTH), 1).astype(jnp.float32)
    filled = jnp.sum(jnp.where(held, 1.0, 0.0), axis=0, keepdims=True)
    value = to_column(value.astype(jnp.float32))
    row = jnp.sum(jnp.where(held, value, 0.0), axis=0, keepdims=True).astype(jnp.int32)
    a, b = iota((KINDS, TILE), 0), iota((KINDS, TILE), 1)
    starts = jnp.sum(jnp.where(a < b, groups, 0.0), axis=0, keepdims=True)
    counts = jnp.sum(jnp.where(a == b, groups, 0.0), axis=0, keepdims=True)
    others = jnp.sum(jnp.where(iota((KINDS, 1), 0) < CLASSES, groups, 0.0)) * GROUP
    is_other = iota((1, WIDTH), 1).astype(jnp.float32) < others
    spare = jnp.where(is_other, OTHER_BLOCKS, OWN_BLOCKS) * 65536
    return jnp.where(filled > 0, row, spare), starts.astype(jnp.int32), counts.astype(jnp.int32)


def plan_kernel(where, dest, source, kept_plan, same_where, plan, sem):
    for i in range(5):
        same_where[i] = where[i]
    my_y, my_x, my_k, my_z, my_xhi = (where[i] for i in range(5))
    block, from_block = dest[...], source[...]
    row = from_block // TPD
    rel = (((row // (NXLO * NCORE)) - my_y) & (NY - 1)) * NXLO
    rel = rel + (((row // NCORE) - my_x) & (NXLO - 1))
    sibling = (row - my_k) & (NCORE - 1)
    slot = jnp.zeros_like(rel)
    for i, (y, x) in enumerate(PACKED):
        slot = jnp.where(rel == y * NXLO + x, i, slot)
    is_far = slot == LAST
    feat = jnp.where(is_far, 0, slot) * TPD + (from_block & (TPD - 1))
    late = jnp.where(slot < EARLY, 0, 1)
    group = jnp.where(is_far, 3 + sibling, jnp.where(sibling == 1, 2, late))
    away, half, inner = split_dest(block, my_z)
    key = away * TPD + inner
    is_own = half == my_xhi
    live = block >= 0
    hit, _, rank = slots_of(key, live & (half != my_xhi))
    slot = jnp.sum(jnp.where(hit, rank, 0.0), axis=0, keepdims=True).astype(jnp.int32)
    to = jnp.where(is_own, key, away * HALF_SLOTS + slot)
    kind = jnp.where(live, jnp.where(is_own, CLASSES, 0) + group, KINDS)
    value = iota((1, SLOTS), 1) + feat * 256 + to * 65536
    row, starts, counts = lists_of(kind, value)
    plan[0:1, :] = row
    plan[1:2, 0:TILE] = starts
    plan[2:3, 0:TILE] = counts
    copy = pltpu.make_async_copy(plan, kept_plan, sem)
    copy.start()
    copy.wait()


def make_plan(where, dest, source):
    return call(
        plan_kernel,
        "plan",
        out_shape=[
            pltpu.SMEM((8, WIDTH), jnp.int32),
            jax.ShapeDtypeStruct(where.shape, where.dtype),
        ],
        in_specs=[SMEM_SPEC] + [VMEM_SPEC] * 2,
        out_specs=[SMEM_SPEC] * 2,
        scratch_shapes=[VMEM((8, WIDTH), jnp.int32), pltpu.SemaphoreType.DMA(())],
    )(where, dest, source)


def map_kernel(where, partner_dest, slots, found, sem):
    my_z, my_xhi = where[3], where[4]
    block = partner_dest[...]
    away, half, inner = split_dest(block, my_z)
    _, touched, rank = slots_of(away * TPD + inner, (block >= 0) & (half == my_xhi))
    slot = to_row(jnp.where(touched > 0, rank, float(HALF_SLOTS)))
    found[...] = slot.astype(jnp.int32)
    copy = pltpu.make_async_copy(found, slots, sem)
    copy.start()
    copy.wait()


def make_map(where, partner_dest):
    return call(
        map_kernel,
        "partner_map",
        out_shape=pltpu.SMEM((1, OWN_BLOCKS), jnp.int32),
        in_specs=[SMEM_SPEC, VMEM_SPEC],
        out_specs=SMEM_SPEC,
        scratch_shapes=[VMEM((1, OWN_BLOCKS), jnp.int32), pltpu.SemaphoreType.DMA(())],
    )(where, partner_dest)


def add_products(plan, kind, tiles, feats, acc):
    def one_group(g, _):
        entries = [plan[0, g * GROUP + i] for i in range(GROUP)]
        products = [
            jnp.dot(
                tiles[e & 255],
                feats[pl.ds(pl.multiple_of(((e >> 8) & 255) * TILE, TILE), TILE), :],
                preferred_element_type=jnp.float32,
            )
            for e in entries
        ]
        for e, product in zip(entries, products):
            acc[e >> 16] += product
        return 0

    first = plan[1, kind]
    lax.fori_loop(first, first + plan[2, kind], one_group, 0)


def clear_blocks(acc, n):
    def clear(i, _):
        acc[i] = jnp.zeros(acc.shape[1:], acc.dtype)
        return 0

    lax.fori_loop(0, n, clear, 0, unroll=4)


def load_tiles_kernel(tiles_hbm, tiles, sem):
    copy = pltpu.make_async_copy(tiles_hbm, tiles, sem)
    copy.start()
    copy.wait()


def load_tiles(tile_set):
    return call(
        load_tiles_kernel,
        "load_tiles",
        out_shape=VMEM(tile_set.shape, tile_set.dtype),
        in_specs=[ANY_SPEC],
        out_specs=VMEM_SPEC,
        scratch_shapes=[pltpu.SemaphoreType.DMA(())],
    )(tile_set)


def pack_kernel(has_base, first, *refs):
    packed = refs[-1]
    for i, ref in enumerate(refs[has_base:-1]):
        packed[pl.ds(first + i * ROWS, ROWS), :] = ref[...]


def pack(base, first, arrays):
    has_base = base is not None
    return call(
        functools.partial(pack_kernel, has_base, first),
        "pack",
        out_shape=VMEM((LAST * ROWS, arrays[0].shape[1]), arrays[0].dtype),
        in_specs=[VMEM_SPEC] * (has_base + len(arrays)),
        out_specs=VMEM_SPEC,
        input_output_aliases={0: 0} if has_base else {},
    )(*([keep(base)] if has_base else []), *arrays)


def pack_second_kernel(_, up_side, down_side, far, packed, *thirds):
    for i, ref in enumerate((far, down_side, up_side)):
        packed[pl.ds((EARLY + i) * ROWS, ROWS), :] = ref[...]
    at = 0
    for n, ref, third in zip(THIRDS, (up_side, down_side, far), thirds):
        third[...] = ref[pl.ds(at, n), :]
        at += n


def pack_second(base, arrays):
    width = base.shape[1]
    packed, *thirds = call(
        pack_second_kernel,
        "pack_second",
        out_shape=[VMEM(base.shape, base.dtype)] + [VMEM((n, width), base.dtype) for n in THIRDS],
        in_specs=[VMEM_SPEC] * 4,
        out_specs=[VMEM_SPEC] * 4,
        input_output_aliases={0: 0},
    )(keep(base), *arrays)
    return packed, thirds


def join_kernel(*refs):
    at = 0
    for ref in refs[:-1]:
        refs[-1][pl.ds(at, ref.shape[0]), :] = ref[...]
        at += ref.shape[0]


def join(arrays):
    return call(
        join_kernel,
        "join",
        out_shape=VMEM((ROWS, arrays[0].shape[1]), arrays[0].dtype),
        in_specs=[VMEM_SPEC] * len(arrays),
        out_specs=VMEM_SPEC,
    )(*arrays)


def first_kernel(plan, tiles, feats, _, other, own):
    clear_blocks(other, OTHER_BLOCKS)
    clear_blocks(own, OWN_BLOCKS)
    add_products(plan, 0, tiles, feats, other)
    add_products(plan, CLASSES, tiles, feats, own)


def first_products(plan, tiles, feats):
    block = (TILE, feats.shape[1])
    return call(
        first_kernel,
        "first_products",
        out_shape=[
            VMEM(feats.shape, feats.dtype),
            VMEM((OTHER_BLOCKS + 1, *block), jnp.float32),
            VMEM((OWN_BLOCKS + 1, *block), jnp.float32),
        ],
        in_specs=[SMEM_SPEC] + [VMEM_SPEC] * 2,
        out_specs=[VMEM_SPEC] * 3,
        input_output_aliases={2: 0},
    )(keep_scalars(plan), keep(tiles), keep(feats))


def more_kernel(kinds, n_feats, plan, tiles, *refs):
    feats, accs = refs[:n_feats], refs[-len(kinds) :]
    for acc, of_acc in zip(accs, kinds):
        for kind, at in of_acc:
            add_products(plan, kind, tiles, feats[at], acc)


def more_products(name, kinds, plan, tiles, feats, accs):
    n = 2 + len(feats)
    return call(
        functools.partial(more_kernel, kinds, len(feats)),
        name,
        out_shape=[VMEM(acc.shape, acc.dtype) for acc in accs],
        in_specs=[SMEM_SPEC] + [VMEM_SPEC] * (n - 1 + len(accs)),
        out_specs=[VMEM_SPEC] * len(accs),
        input_output_aliases={n + i: i for i in range(len(accs))},
    )(keep_scalars(plan), keep(tiles), *[keep(f) for f in feats], *[keep(acc) for acc in accs])


def convert_sends(acc, parts, sends):
    for aways, send in zip(parts, sends):
        for i, away in enumerate(aways):
            blocks = acc[pl.ds(away * HALF_SLOTS, HALF_SLOTS)]
            send[pl.ds(i * HALF_SLOTS, HALF_SLOTS)] = blocks.astype(send.dtype)


def first_send_kernel(plan, tiles, far_sibling, _, acc, send):
    add_products(plan, 4, tiles, far_sibling, acc)
    convert_sends(acc, X_PARTS[:1], [send])


def sends_kernel(acc, *sends):
    convert_sends(acc, X_PARTS[1:], sends)


def make_sends(plan, tiles, far_sibling, acc):
    part = lambda p: VMEM((HALF_SLOTS * len(p), *acc.shape[1:]), jnp.bfloat16)
    acc, first = call(
        first_send_kernel,
        "first_send",
        out_shape=[VMEM(acc.shape, acc.dtype), part(X_PARTS[0])],
        in_specs=[SMEM_SPEC] + [VMEM_SPEC] * 3,
        out_specs=[VMEM_SPEC] * 2,
        input_output_aliases={3: 0},
    )(keep_scalars(plan), keep(tiles), keep(far_sibling), keep(acc))
    rest = call(
        sends_kernel,
        "other_sends",
        out_shape=[part(p) for p in X_PARTS[1:]],
        in_specs=[VMEM_SPEC],
        out_specs=[VMEM_SPEC] * (len(X_PARTS) - 1),
    )(keep(acc))
    return [first, *rest]


def merged(away, first, slots, own, arrived, passed, i):
    total = own[away * TPD + i]
    for ref, at in passed:
        if at <= i < at + ref.shape[0]:
            total += ref[i - at].astype(jnp.float32)
    slot = slots[0, away * TPD + i]
    seen = (slot < HALF_SLOTS).astype(jnp.float32)
    block = arrived[first + jnp.minimum(slot, HALF_SLOTS - 1)]
    return total + block.astype(jnp.float32) * seen


def hop_kernel(parts, slots, own, arrived, *refs):
    passed, outs = refs[: -len(parts)], refs[-len(parts) :]
    for out, (away, first, n, at, pass_at) in zip(outs, parts):
        refs = [(passed[i], block) for i, block in pass_at]
        for i in range(n):
            total = merged(away, first, slots, own, arrived, refs, at + i)
            out[i] = total.astype(out.dtype)


def hop(name, parts, slots, own, arrived, passed=()):
    return call(
        functools.partial(hop_kernel, parts),
        name,
        out_shape=[VMEM((p[2], *own.shape[1:]), jnp.bfloat16) for p in parts],
        in_specs=[SMEM_SPEC] + [VMEM_SPEC] * (2 + len(passed)),
        out_specs=[VMEM_SPEC] * len(parts),
    )(keep_scalars(slots), keep(own), arrived, *passed)


def last_kernel(first, slots, own, arrived, passed_a, passed_b, weight, bias, out):
    passed = [(passed_a, 0), (passed_b, 0)]
    for i in range(TPD):
        total = merged(0, first, slots, own, arrived, passed, i).astype(jnp.bfloat16)
        hidden = jnp.dot(total, weight[...], preferred_element_type=jnp.float32) + bias[...]
        out[pl.ds(i * TILE, TILE), :] = jnp.maximum(hidden, 0.0).astype(out.dtype)


def last(slots, own, arrived, passed, weight, bias):
    part, first = arrived
    return call(
        functools.partial(last_kernel, first),
        "last",
        out_shape=jax.ShapeDtypeStruct((ROWS, weight.shape[1]), jnp.bfloat16),
        in_specs=[SMEM_SPEC] + [VMEM_SPEC] * (4 + len(passed)),
        out_specs=VMEM_SPEC,
    )(keep_scalars(slots), keep(own), part, *passed, weight, bias)


def send(array, perm):
    return lax.ppermute(array, "row", perm)


def on_device(node_feats, tile_vals, tile_dest, tile_source, tile_count, weight, out_bias):
    row, col = lax.axis_index("row"), lax.axis_index("col")
    where = jnp.stack(
        [row // (NXLO * NCORE), row // NCORE % NXLO, row % NCORE, col // NXHI, col % NXHI]
    ).astype(jnp.int32)
    slot = jnp.arange(SLOTS, dtype=jnp.int32)[None, :]
    dest = jnp.where(slot < tile_count[0, 0], tile_dest[0], -1)
    up, down, side = (send(node_feats, p) for p in (FROM_UP, FROM_DOWN, FROM_SIDE))
    plan, where = make_plan(where, dest, tile_source[0])
    up, down, side, where = lax.optimization_barrier((up, down, side, where))
    far, down_side, up_side = send(up, FROM_UP), send(side, FROM_DOWN), send(up, FROM_SIDE)
    tiles = load_tiles(tile_vals[0, 0])
    feats = pack(None, 0, [node_feats, up, down, side])
    feats, other, own = first_products(plan, tiles, feats)
    far, down_side, up_side, feats, other, own = lax.optimization_barrier(
        (far, down_side, up_side, feats, other, own)
    )
    partner_dest = lax.ppermute(dest, "col", X_FLIP)
    feats, parts = pack_second(feats, (up_side, down_side, far))
    thirds = [send(p, perm) for p, perm in zip(parts, (FROM_UP, FROM_DOWN, FROM_SIDE))]
    sibling = send(feats, FROM_CORE)
    kinds = (((1, 0),), ((CLASSES + 1, 0),))
    other, own = more_products("late_products", kinds, plan, tiles, [feats], [other, own])
    thirds, other, own, partner_dest = lax.optimization_barrier((thirds, other, own, partner_dest))
    slots = make_map(where, partner_dest)
    last_feats = join(thirds)
    far_sibling = send(last_feats, FROM_CORE)
    kinds = (((2, 0), (3, 1)),)
    (other,) = more_products("other_half", kinds, plan, tiles, [sibling, last_feats], [other])
    sends = make_sends(plan, tiles, far_sibling, other)
    arrived = {}
    for aways, part in zip(X_PARTS, sends):
        part = lax.ppermute(part, "col", X_FLIP)
        for i, away in enumerate(aways):
            arrived[away] = (part, i * HALF_SLOTS)
    kinds = (tuple((CLASSES + 2 + i, i) for i in range(3)),)
    rest = [sibling, last_feats, far_sibling]
    (own,) = more_products("own_half", kinds, plan, tiles, rest, [own])
    cut = TPD // 2
    parts = ((4, 0, cut, 0, ()), (4, 0, cut, cut, ()))
    chains = hop("hop_4", parts, slots, own, arrived[4][0])
    for a, b in ((3, 5), (2, 6), (1, 7)):
        chains = [lax.ppermute(c, "col", p) for c, p in zip(chains, Z_CHAINS)]
        at = (0, cut if a == 3 else 0)
        chains = [
            hop(
                f"hop_{away}",
                ((away, arrived[away][1], TPD, 0, ((0, at[i]),)),),
                slots,
                own,
                arrived[away][0],
                (c,),
            )[0]
            for i, (away, c) in enumerate(zip((a, b), chains))
        ]
    chains = [lax.ppermute(c, "col", p) for c, p in zip(chains, Z_CHAINS)]
    return last(slots, own, arrived[0], chains, weight, out_bias.reshape(1, -1))


def solution(mesh):
    return jax.shard_map(
        on_device,
        mesh=mesh,
        in_specs=(
            P(("row", "col"), None),
            P("row", "col", None, None, None),
            P("row", "col", None),
            P("row", "col", None),
            P("row", "col"),
            P(),
            P(),
        ),
        out_specs=P(("row", "col"), None),
        check_vma=False,
    )
```

```python
import functools

import jax
import jax.numpy as jnp
from jax import lax
from jax.experimental import pallas as pl
from jax.experimental.pallas import tpu as pltpu
from jax.sharding import PartitionSpec as P

TILE = 128
TPD = 16
SLOTS = 256
NY, NXLO, NCORE = 4, 2, 2
NZ, NXHI = 8, 2
ROWS = TPD * TILE
HALF_SLOTS = 8
OWN_BLOCKS = NZ * TPD
OTHER_BLOCKS = NZ * HALF_SLOTS
GROUP = 16
WIDTH = 512
CLASSES = 5
KINDS = 16
PACKED = ((0, 0), (1, 0), (3, 0), (0, 1), (2, 0), (3, 1), (1, 1), (2, 1))
EARLY = 4
LAST = 7
X_PARTS = ((4,), (3,), (5,), (2, 6), (1, 7), (0,))
THIRDS = (752, 880, 416)

VMEM = pltpu.VMEM
SMEM_SPEC = pl.BlockSpec(memory_space=pltpu.SMEM)
VMEM_SPEC = pl.BlockSpec(memory_space=pltpu.VMEM)
ANY_SPEC = pl.BlockSpec(memory_space=pl.ANY)


def row_perm(change):
    pairs = []
    for y in range(NY):
        for x in range(NXLO):
            for k in range(NCORE):
                ty, tx, tk = change(y, x, k)
                pairs.append(((y * NXLO + x) * NCORE + k, (ty % NY * NXLO + tx) * NCORE + tk))
    return pairs


FROM_UP = row_perm(lambda y, x, k: (y - 1, x, k))
FROM_DOWN = row_perm(lambda y, x, k: (y + 1, x, k))
FROM_SIDE = row_perm(lambda y, x, k: (y, 1 - x, k))
FROM_CORE = row_perm(lambda y, x, k: (y, x, 1 - k))
Z_PLUS = [(z * NXHI + x, (z + 1) % NZ * NXHI + x) for z in range(NZ) for x in range(NXHI)]
Z_MINUS = [(z * NXHI + x, (z - 1) % NZ * NXHI + x) for z in range(NZ) for x in range(NXHI)]
Z_CHAINS = (Z_PLUS, Z_MINUS)
X_FLIP = [(z * NXHI + x, z * NXHI + 1 - x) for z in range(NZ) for x in range(NXHI)]


def call(kernel, name, **kwargs):
    return pl.pallas_call(
        kernel,
        name=name,
        cost_estimate=pl.CostEstimate(flops=0, bytes_accessed=0, transcendentals=0),
        compiler_params=pltpu.CompilerParams(vmem_limit_bytes=16 << 20),
        **kwargs,
    )


def keep_scalars(array):
    return pltpu.with_memory_space_constraint(array, pltpu.SMEM)


def keep(array):
    return pltpu.with_memory_space_constraint(array, pltpu.VMEM)


def iota(shape, dim):
    return lax.broadcasted_iota(jnp.int32, shape, dim)


def to_column(row):
    n = row.shape[1]
    square = jnp.broadcast_to(row, (n, n))
    return jnp.sum(jnp.where(iota((n, n), 0) == iota((n, n), 1), square, 0.0), 1, keepdims=True)


def to_row(column):
    n = column.shape[0]
    square = jnp.broadcast_to(column, (n, n))
    return jnp.sum(jnp.where(iota((n, n), 0) == iota((n, n), 1), square, 0.0), 0, keepdims=True)


def split_dest(block, my_z):
    block = jnp.maximum(block, 0)
    away = ((block // (NXHI * TPD)) - my_z) & (NZ - 1)
    return away, (block // TPD) & (NXHI - 1), block & (TPD - 1)


def slots_of(key, chosen):
    hit = (iota((OWN_BLOCKS, SLOTS), 0) == key) & chosen
    touched = jnp.max(jnp.where(hit, 1.0, 0.0), axis=1, keepdims=True)
    a, b = iota((OWN_BLOCKS, OWN_BLOCKS), 0), iota((OWN_BLOCKS, OWN_BLOCKS), 1)
    before = (b < a) & (b // TPD == a // TPD)
    rank = jnp.sum(jnp.where(before, to_row(touched), 0.0), axis=1, keepdims=True)
    return hit, touched, rank


def lists_of(kind, value):
    kinds = iota((KINDS, SLOTS), 0)
    n = jnp.sum(jnp.where(kinds == kind, 1, 0).astype(jnp.float32), axis=1, keepdims=True)
    groups = jnp.floor((n + (GROUP - 1)) * (1.0 / GROUP))
    first = jnp.sum(jnp.where(kinds < kind, groups, 0.0), axis=0, keepdims=True) * GROUP
    kind_column = to_column(kind.astype(jnp.float32))
    earlier = iota((SLOTS, SLOTS), 0) < iota((SLOTS, SLOTS), 1)
    same = (kind_column == kind.astype(jnp.float32)) & earlier
    at = first + jnp.sum(jnp.where(same, 1.0, 0.0), axis=0, keepdims=True)
    at = to_column(jnp.where(kind < KINDS, at, -1.0))
    held = at == iota((SLOTS, WIDTH), 1).astype(jnp.float32)
    filled = jnp.sum(jnp.where(held, 1.0, 0.0), axis=0, keepdims=True)
    value = to_column(value.astype(jnp.float32))
    row = jnp.sum(jnp.where(held, value, 0.0), axis=0, keepdims=True).astype(jnp.int32)
    a, b = iota((KINDS, TILE), 0), iota((KINDS, TILE), 1)
    starts = jnp.sum(jnp.where(a < b, groups, 0.0), axis=0, keepdims=True)
    counts = jnp.sum(jnp.where(a == b, groups, 0.0), axis=0, keepdims=True)
    others = jnp.sum(jnp.where(iota((KINDS, 1), 0) < CLASSES, groups, 0.0)) * GROUP
    is_other = iota((1, WIDTH), 1).astype(jnp.float32) < others
    spare = jnp.where(is_other, OTHER_BLOCKS, OWN_BLOCKS) * 65536
    return jnp.where(filled > 0, row, spare), starts.astype(jnp.int32), counts.astype(jnp.int32)


def plan_kernel(where, dest, source, kept_plan, same_where, plan, sem):
    for i in range(5):
        same_where[i] = where[i]
    my_y, my_x, my_k, my_z, my_xhi = (where[i] for i in range(5))
    block, from_block = dest[...], source[...]
    row = from_block // TPD
    rel = (((row // (NXLO * NCORE)) - my_y) & (NY - 1)) * NXLO
    rel = rel + (((row // NCORE) - my_x) & (NXLO - 1))
    sibling = (row - my_k) & (NCORE - 1)
    slot = jnp.zeros_like(rel)
    for i, (y, x) in enumerate(PACKED):
        slot = jnp.where(rel == y * NXLO + x, i, slot)
    is_far = slot == LAST
    feat = jnp.where(is_far, 0, slot) * TPD + (from_block & (TPD - 1))
    late = jnp.where(slot < EARLY, 0, 1)
    group = jnp.where(is_far, 3 + sibling, jnp.where(sibling == 1, 2, late))
    away, half, inner = split_dest(block, my_z)
    key = away * TPD + inner
    is_own = half == my_xhi
    live = block >= 0
    hit, _, rank = slots_of(key, live & (half != my_xhi))
    slot = jnp.sum(jnp.where(hit, rank, 0.0), axis=0, keepdims=True).astype(jnp.int32)
    to = jnp.where(is_own, key, away * HALF_SLOTS + slot)
    kind = jnp.where(live, jnp.where(is_own, CLASSES, 0) + group, KINDS)
    value = iota((1, SLOTS), 1) + feat * 256 + to * 65536
    row, starts, counts = lists_of(kind, value)
    plan[0:1, :] = row
    plan[1:2, 0:TILE] = starts
    plan[2:3, 0:TILE] = counts
    copy = pltpu.make_async_copy(plan, kept_plan, sem)
    copy.start()
    copy.wait()


def make_plan(where, dest, source):
    return call(
        plan_kernel,
        "plan",
        out_shape=[
            pltpu.SMEM((8, WIDTH), jnp.int32),
            jax.ShapeDtypeStruct(where.shape, where.dtype),
        ],
        in_specs=[SMEM_SPEC] + [VMEM_SPEC] * 2,
        out_specs=[SMEM_SPEC] * 2,
        scratch_shapes=[VMEM((8, WIDTH), jnp.int32), pltpu.SemaphoreType.DMA(())],
    )(where, dest, source)


def map_kernel(where, partner_dest, slots, found, sem):
    my_z, my_xhi = where[3], where[4]
    block = partner_dest[...]
    away, half, inner = split_dest(block, my_z)
    _, touched, rank = slots_of(away * TPD + inner, (block >= 0) & (half == my_xhi))
    slot = to_row(jnp.where(touched > 0, rank, float(HALF_SLOTS)))
    found[...] = slot.astype(jnp.int32)
    copy = pltpu.make_async_copy(found, slots, sem)
    copy.start()
    copy.wait()


def make_map(where, partner_dest):
    return call(
        map_kernel,
        "partner_map",
        out_shape=pltpu.SMEM((1, OWN_BLOCKS), jnp.int32),
        in_specs=[SMEM_SPEC, VMEM_SPEC],
        out_specs=SMEM_SPEC,
        scratch_shapes=[VMEM((1, OWN_BLOCKS), jnp.int32), pltpu.SemaphoreType.DMA(())],
    )(where, partner_dest)


def add_products(plan, kind, tiles, feats, acc):
    def one_group(g, _):
        entries = [plan[0, g * GROUP + i] for i in range(GROUP)]
        products = [
            jnp.dot(
                tiles[e & 255],
                feats[pl.ds(pl.multiple_of(((e >> 8) & 255) * TILE, TILE), TILE), :],
                preferred_element_type=jnp.float32,
            )
            for e in entries
        ]
        for e, product in zip(entries, products):
            acc[e >> 16] += product
        return 0

    first = plan[1, kind]
    lax.fori_loop(first, first + plan[2, kind], one_group, 0)


def clear_blocks(acc, n):
    def clear(i, _):
        acc[i] = jnp.zeros(acc.shape[1:], acc.dtype)
        return 0

    lax.fori_loop(0, n, clear, 0, unroll=4)


def load_tiles_kernel(tiles_hbm, tiles, sem):
    copy = pltpu.make_async_copy(tiles_hbm, tiles, sem)
    copy.start()
    copy.wait()


def load_tiles(tile_set):
    return call(
        load_tiles_kernel,
        "load_tiles",
        out_shape=VMEM(tile_set.shape, tile_set.dtype),
        in_specs=[ANY_SPEC],
        out_specs=VMEM_SPEC,
        scratch_shapes=[pltpu.SemaphoreType.DMA(())],
    )(tile_set)


def pack_kernel(has_base, first, *refs):
    packed = refs[-1]
    for i, ref in enumerate(refs[has_base:-1]):
        packed[pl.ds(first + i * ROWS, ROWS), :] = ref[...]


def pack(base, first, arrays):
    has_base = base is not None
    return call(
        functools.partial(pack_kernel, has_base, first),
        "pack",
        out_shape=VMEM((LAST * ROWS, arrays[0].shape[1]), arrays[0].dtype),
        in_specs=[VMEM_SPEC] * (has_base + len(arrays)),
        out_specs=VMEM_SPEC,
        input_output_aliases={0: 0} if has_base else {},
    )(*([keep(base)] if has_base else []), *arrays)


def pack_second_kernel(_, up_side, down_side, far, packed, *thirds):
    for i, ref in enumerate((far, down_side, up_side)):
        packed[pl.ds((EARLY + i) * ROWS, ROWS), :] = ref[...]
    at = 0
    for n, ref, third in zip(THIRDS, (up_side, down_side, far), thirds):
        third[...] = ref[pl.ds(at, n), :]
        at += n


def pack_second(base, arrays):
    width = base.shape[1]
    packed, *thirds = call(
        pack_second_kernel,
        "pack_second",
        out_shape=[VMEM(base.shape, base.dtype)] + [VMEM((n, width), base.dtype) for n in THIRDS],
        in_specs=[VMEM_SPEC] * 4,
        out_specs=[VMEM_SPEC] * 4,
        input_output_aliases={0: 0},
    )(keep(base), *arrays)
    return packed, thirds


def join_kernel(*refs):
    at = 0
    for ref in refs[:-1]:
        refs[-1][pl.ds(at, ref.shape[0]), :] = ref[...]
        at += ref.shape[0]


def join(arrays):
    return call(
        join_kernel,
        "join",
        out_shape=VMEM((ROWS, arrays[0].shape[1]), arrays[0].dtype),
        in_specs=[VMEM_SPEC] * len(arrays),
        out_specs=VMEM_SPEC,
    )(*arrays)


def first_kernel(plan, tiles, feats, _, other, own):
    clear_blocks(other, OTHER_BLOCKS)
    clear_blocks(own, OWN_BLOCKS)
    add_products(plan, 0, tiles, feats, other)
    add_products(plan, CLASSES, tiles, feats, own)


def first_products(plan, tiles, feats):
    block = (TILE, feats.shape[1])
    return call(
        first_kernel,
        "first_products",
        out_shape=[
            VMEM(feats.shape, feats.dtype),
            VMEM((OTHER_BLOCKS + 1, *block), jnp.float32),
            VMEM((OWN_BLOCKS + 1, *block), jnp.float32),
        ],
        in_specs=[SMEM_SPEC] + [VMEM_SPEC] * 2,
        out_specs=[VMEM_SPEC] * 3,
        input_output_aliases={2: 0},
    )(keep_scalars(plan), keep(tiles), keep(feats))


def more_kernel(kinds, n_feats, plan, tiles, *refs):
    feats, accs = refs[:n_feats], refs[-len(kinds) :]
    for acc, of_acc in zip(accs, kinds):
        for kind, at in of_acc:
            add_products(plan, kind, tiles, feats[at], acc)


def more_products(name, kinds, plan, tiles, feats, accs):
    n = 2 + len(feats)
    return call(
        functools.partial(more_kernel, kinds, len(feats)),
        name,
        out_shape=[VMEM(acc.shape, acc.dtype) for acc in accs],
        in_specs=[SMEM_SPEC] + [VMEM_SPEC] * (n - 1 + len(accs)),
        out_specs=[VMEM_SPEC] * len(accs),
        input_output_aliases={n + i: i for i in range(len(accs))},
    )(keep_scalars(plan), keep(tiles), *[keep(f) for f in feats], *[keep(acc) for acc in accs])


def convert_sends(acc, parts, sends):
    for aways, send in zip(parts, sends):
        for i, away in enumerate(aways):
            blocks = acc[pl.ds(away * HALF_SLOTS, HALF_SLOTS)]
            send[pl.ds(i * HALF_SLOTS, HALF_SLOTS)] = blocks.astype(send.dtype)


def first_send_kernel(plan, tiles, far_sibling, _, acc, send):
    add_products(plan, 4, tiles, far_sibling, acc)
    convert_sends(acc, X_PARTS[:1], [send])


def sends_kernel(acc, *sends):
    convert_sends(acc, X_PARTS[1:], sends)


def make_sends(plan, tiles, far_sibling, acc):
    part = lambda p: VMEM((HALF_SLOTS * len(p), *acc.shape[1:]), jnp.bfloat16)
    acc, first = call(
        first_send_kernel,
        "first_send",
        out_shape=[VMEM(acc.shape, acc.dtype), part(X_PARTS[0])],
        in_specs=[SMEM_SPEC] + [VMEM_SPEC] * 3,
        out_specs=[VMEM_SPEC] * 2,
        input_output_aliases={3: 0},
    )(keep_scalars(plan), keep(tiles), keep(far_sibling), keep(acc))
    rest = call(
        sends_kernel,
        "other_sends",
        out_shape=[part(p) for p in X_PARTS[1:]],
        in_specs=[VMEM_SPEC],
        out_specs=[VMEM_SPEC] * (len(X_PARTS) - 1),
    )(keep(acc))
    return [first, *rest]


def merged(away, first, slots, own, arrived, passed, i):
    total = own[away * TPD + i]
    for ref, at in passed:
        if at <= i < at + ref.shape[0]:
            total += ref[i - at].astype(jnp.float32)
    slot = slots[0, away * TPD + i]
    seen = (slot < HALF_SLOTS).astype(jnp.float32)
    block = arrived[first + jnp.minimum(slot, HALF_SLOTS - 1)]
    return total + block.astype(jnp.float32) * seen


def hop_kernel(parts, slots, own, arrived, *refs):
    passed, outs = refs[: -len(parts)], refs[-len(parts) :]
    for out, (away, first, n, at, pass_at) in zip(outs, parts):
        refs = [(passed[i], block) for i, block in pass_at]
        for i in range(n):
            total = merged(away, first, slots, own, arrived, refs, at + i)
            out[i] = total.astype(out.dtype)


def hop(name, parts, slots, own, arrived, passed=()):
    return call(
        functools.partial(hop_kernel, parts),
        name,
        out_shape=[VMEM((p[2], *own.shape[1:]), jnp.bfloat16) for p in parts],
        in_specs=[SMEM_SPEC] + [VMEM_SPEC] * (2 + len(passed)),
        out_specs=[VMEM_SPEC] * len(parts),
    )(keep_scalars(slots), keep(own), arrived, *passed)


def last_kernel(first, slots, own, arrived, passed_a, passed_b, weight, bias, out, held, sems):
    rows = ROWS // 4

    def copy_out(j):
        at = pl.ds(j * rows, rows)
        return pltpu.make_async_copy(held.at[at], out.at[at], sems.at[j])

    passed = [(passed_a, 0), (passed_b, 0)]
    for i in range(TPD):
        total = merged(0, first, slots, own, arrived, passed, i).astype(jnp.bfloat16)
        hidden = jnp.dot(total, weight[...], preferred_element_type=jnp.float32) + bias[...]
        held[pl.ds(i * TILE, TILE), :] = jnp.maximum(hidden, 0.0).astype(held.dtype)
        if (i + 1) * TILE % rows == 0:
            copy_out(i * TILE // rows).start()
    for j in range(4):
        copy_out(j).wait()


def last(slots, own, arrived, passed, weight, bias):
    part, first = arrived
    return call(
        functools.partial(last_kernel, first),
        "last",
        out_shape=jax.ShapeDtypeStruct((ROWS, weight.shape[1]), jnp.bfloat16),
        in_specs=[SMEM_SPEC] + [VMEM_SPEC] * (4 + len(passed)),
        out_specs=ANY_SPEC,
        scratch_shapes=[
            VMEM((ROWS, weight.shape[1]), jnp.bfloat16),
            pltpu.SemaphoreType.DMA((4,)),
        ],
    )(keep_scalars(slots), keep(own), part, *passed, weight, bias)


def send(array, perm):
    return lax.ppermute(array, "row", perm)


def on_device(node_feats, tile_vals, tile_dest, tile_source, tile_count, weight, out_bias):
    row, col = lax.axis_index("row"), lax.axis_index("col")
    where = jnp.stack(
        [row // (NXLO * NCORE), row // NCORE % NXLO, row % NCORE, col // NXHI, col % NXHI]
    ).astype(jnp.int32)
    slot = jnp.arange(SLOTS, dtype=jnp.int32)[None, :]
    dest = jnp.where(slot < tile_count[0, 0], tile_dest[0], -1)
    up, down, side = (send(node_feats, p) for p in (FROM_UP, FROM_DOWN, FROM_SIDE))
    plan, where = make_plan(where, dest, tile_source[0])
    up, down, side, where = lax.optimization_barrier((up, down, side, where))
    far, down_side, up_side = send(up, FROM_UP), send(side, FROM_DOWN), send(up, FROM_SIDE)
    tiles = load_tiles(tile_vals[0, 0])
    feats = pack(None, 0, [node_feats, up, down, side])
    feats, other, own = first_products(plan, tiles, feats)
    far, down_side, up_side, feats, other, own = lax.optimization_barrier(
        (far, down_side, up_side, feats, other, own)
    )
    partner_dest = lax.ppermute(dest, "col", X_FLIP)
    feats, parts = pack_second(feats, (up_side, down_side, far))
    thirds = [send(p, perm) for p, perm in zip(parts, (FROM_UP, FROM_DOWN, FROM_SIDE))]
    sibling = send(feats, FROM_CORE)
    kinds = (((1, 0),), ((CLASSES + 1, 0),))
    other, own = more_products("late_products", kinds, plan, tiles, [feats], [other, own])
    thirds, other, own, partner_dest = lax.optimization_barrier((thirds, other, own, partner_dest))
    slots = make_map(where, partner_dest)
    last_feats = join(thirds)
    far_sibling = send(last_feats, FROM_CORE)
    kinds = (((2, 0), (3, 1)),)
    (other,) = more_products("other_half", kinds, plan, tiles, [sibling, last_feats], [other])
    sends = make_sends(plan, tiles, far_sibling, other)
    arrived = {}
    for aways, part in zip(X_PARTS, sends):
        part = lax.ppermute(part, "col", X_FLIP)
        for i, away in enumerate(aways):
            arrived[away] = (part, i * HALF_SLOTS)
    kinds = (tuple((CLASSES + 2 + i, i) for i in range(3)),)
    rest = [sibling, last_feats, far_sibling]
    (own,) = more_products("own_half", kinds, plan, tiles, rest, [own])
    cut = TPD // 2
    parts = ((4, 0, cut, 0, ()), (4, 0, cut, cut, ()))
    chains = hop("hop_4", parts, slots, own, arrived[4][0])
    for a, b in ((3, 5), (2, 6), (1, 7)):
        chains = [lax.ppermute(c, "col", p) for c, p in zip(chains, Z_CHAINS)]
        at = (0, cut if a == 3 else 0)
        chains = [
            hop(
                f"hop_{away}",
                ((away, arrived[away][1], TPD, 0, ((0, at[i]),)),),
                slots,
                own,
                arrived[away][0],
                (c,),
            )[0]
            for i, (away, c) in enumerate(zip((a, b), chains))
        ]
    chains = [lax.ppermute(c, "col", p) for c, p in zip(chains, Z_CHAINS)]
    return last(slots, own, arrived[0], chains, weight, out_bias.reshape(1, -1))


def solution(mesh):
    return jax.shard_map(
        on_device,
        mesh=mesh,
        in_specs=(
            P(("row", "col"), None),
            P("row", "col", None, None, None),
            P("row", "col", None),
            P("row", "col", None),
            P("row", "col"),
            P(),
            P(),
        ),
        out_specs=P(("row", "col"), None),
        check_vma=False,
    )
```
